256 devices in a mesh: ex: 64 (over y, z, core), rep: 4 (over x).
Axes of the slice: x: 4, y: 4, z: 8, core: 2. Of those that a mesh axis runs over, the one named last changes fastest.
Arguments:
- embeddings: bfloat16 [393216, 1024], P(('ex', 'rep')), may hold values from -6 to 6
- block_rows: bfloat16 [98304, 1024], P(('ex', 'rep')), may hold values from -6 to 6
- owners: int32 [98304, 1], P(('ex', 'rep')), may hold values from 0 to 63; in each aligned block of 384 rows (0 to 383, 384 to 767, ...) at most 12 rows name the same one
- query_cluster: int32 [98304], P(('ex', 'rep')), may hold values from 0 to 7
- member_cluster: int32 [64, 6144], P('ex', 'rep'), may hold values from 0 to 7, never falling along the last dimension, each value on 1 to 1536 neighbouring positions
Outputs:
- query_max: float32 [98304], P(('ex', 'rep'))
- resident_max: float32 [393216], P(('ex', 'rep'))
The draws below stay inside these ranges and needn't reach their ends.
Inputs may be any that keep to these rules, and one draw needn't show every extreme that they name: `owners`: among the rows of one device each group is named by at most 12 rows, a bound that some block reaches. `member_cluster`: nondecreasing along each group's row; each of the 8 clusters has at least one member in every group.
All inputs are finite; a program needn't handle non-finite values.
Results may differ from the reference program's by a relative error of at most 0.0016.
Values may be sent and summed in bfloat16 or wider, within the bound.
A program may use at most 64 MiB of HBM per device.

```python
import math
import jax
import jax.numpy as jnp
import numpy as np
from jax import lax

D = 1024
Q = 384
CPG = 8
CAP = 12
GROUP_ROWS = 6144
ROWS = 393216
QUERIES = 98304
N_EX = 64
N_REP = 4


def place_ends(drawn, own_key, low, high):
    spot = [jax.random.randint(jax.random.fold_in(own_key, axis), (), 0, length) for axis, length in enumerate(drawn.shape)]
    main_axis = drawn.shape.index(max(drawn.shape))
    beside = spot[:main_axis] + [(spot[main_axis] + 1) % drawn.shape[main_axis]] + spot[main_axis + 1:]
    return drawn.at[tuple(spot)].set(low).at[tuple(beside)].set(high)


def block_scale(stream_key, extent, pieces, smallest, top_value):
    factor_of = 1.0
    for position, blocks in pieces:
        heights = jax.random.uniform(jax.random.fold_in(jax.random.fold_in(stream_key, 6), position), (blocks,), jnp.float32, smallest / len(pieces), top_value / len(pieces))
        factor_of = factor_of * jnp.repeat(jnp.exp(heights), extent[position] // blocks).reshape((-1,) + (1,) * (len(extent) - 1 - position))
    return factor_of


def profile(amount, total, reach, slope):
    weights = [(1 << 20) // math.isqrt(standing ** slope) + 1 for standing in range(2, amount + 1)]
    spare, counts = total - reach - (amount - 1), [1] * (amount - 1)
    while spare > 0:
        candidates = [i for i in range(amount - 1) if counts[i] < reach]
        whole, remaining = sum([weights[i] for i in candidates]), spare
        for i in candidates:
            extra = min(reach - counts[i], max(1, remaining * weights[i] // whole), spare)
            counts[i] = counts[i] + extra
            spare = spare - extra
    return np.array([reach] + counts)


def uneven_parts(stream_key, count, total, limit, lean):
    if count == 2:
        one = jax.random.randint(stream_key, (), max(1, total - limit), min(limit, total - 1) + 1)
        return jnp.stack([one, total - one])
    lengths = jnp.asarray(profile(count, total, limit, lean), jnp.int32)
    pairs = (count - 1) // 2
    source_of, receiver = lengths[1:1 + 2 * pairs:2], lengths[2:2 + 2 * pairs:2]
    slack = jnp.minimum(source_of - 1, limit - receiver)
    moved = jax.random.randint(jax.random.fold_in(stream_key, 1), (pairs,), 0, 1 << 20) % (slack + 1)
    lengths = lengths.at[1:1 + 2 * pairs:2].set(source_of - moved).at[2:2 + 2 * pairs:2].set(receiver + moved)
    return lengths[jax.random.permutation(jax.random.fold_in(stream_key, 2), count)]


def routed_block(stream_key, own, number, rows, count, top, limit, lean):
    ranking = jax.random.permutation(stream_key, count)
    heavy_load, common = portions_of(count, rows * top, limit, lean, True), portions_of(count, rows * top, limit, lean, False)
    places = jnp.arange(count)

    def named(lengths, turn):
        used = int((lengths > 0).sum())
        fixed = max(1, used // 4)
        shifted = fixed + (places - fixed + turn * (used - fixed)) % max(1, count - fixed)
        return jnp.zeros((count,), jnp.int32).at[ranking[jnp.where(places < fixed, places, shifted)]].set(jnp.asarray(lengths, jnp.int32))

    lengths = jnp.where(number % 4 == 0, named(heavy_load, number // 4), named(common, number - number // 4 - 1))
    mixed = jax.random.permutation(jax.random.fold_in(own, 3), count)
    giver, sink = mixed[0:count // 2 * 2:2], mixed[1:count // 2 * 2:2]
    margin = jnp.minimum(lengths[giver] - 1, limit - lengths[sink]) // 2
    margin = jnp.where((giver == ranking[0]) | (sink == ranking[0]) | (lengths[sink] == 0), 0, jnp.maximum(margin, 0))
    shifted = jax.random.randint(jax.random.fold_in(own, 4), (count // 2,), 0, 1 << 20) % (margin + 1)
    lengths = lengths.at[giver].add(-shifted).at[sink].add(shifted)
    items = jnp.searchsorted(jnp.cumsum(lengths), jnp.arange(rows * top), side="right").astype(jnp.int32)
    grid = items.reshape(top, rows).T
    grid = grid[jax.random.permutation(jax.random.fold_in(own, 1), rows)]
    turn = jax.random.randint(jax.random.fold_in(own, 2), (rows, 1), 0, top)
    return jnp.take_along_axis(grid, (jnp.arange(top)[None, :] + turn) % top, axis=1)


def portions_of(count, total, most, slope, full):
    loads = [(1 << 20) // math.isqrt(standing ** slope) + 1 for standing in range(1, count + 1)]
    largest = most if full else min(most, max(-(-total // count), total * loads[0] // sum(loads)))
    least = 1 if total - largest >= count - 1 else 0
    counts, rest = [largest] + [least] * (count - 1), total - largest - least * (count - 1)
    while rest > 0:
        movable = [i for i in range(1, count) if counts[i] < largest] or [i for i in range(1, count) if counts[i] < most]
        whole, left = sum([loads[i] for i in movable]), rest
        for i in movable:
            addition = min(most - counts[i], max(1, left * loads[i] // whole), rest)
            counts[i] = counts[i] + addition
            rest = rest - addition
    return np.array(counts)


def normal_values(rng, shape, deviation, most, cuts=(), kind=jnp.bfloat16):
    gain = block_scale(rng, shape, cuts, -0.22, 0.18) if cuts else 1.0
    drawn = jax.random.normal(rng, shape, jnp.float32) * deviation * gain
    return jnp.minimum(jnp.maximum(drawn, -most), most).astype(kind)


def setup_inputs(seed: int = 0) -> dict:
    key_of = jax.random.split(jax.random.key(seed), 6)
    embeddings = normal_values(key_of[0], (ROWS, D), 1.0, 6.0, ((0, 256),))
    block_rows = normal_values(key_of[1], (QUERIES, D), 1.0, 6.0, ((0, 256),))
    owners_keys = jax.random.split(jax.random.fold_in(key_of[2], 1), QUERIES // Q)
    owners_turns = jax.random.permutation(jax.random.fold_in(key_of[2], 3), QUERIES // Q)
    owners = jax.vmap(lambda own, number: routed_block(jax.random.fold_in(key_of[2], 2), own, number, Q, N_EX, 1, CAP, 2))(owners_keys, owners_turns).reshape((QUERIES, 1))
    query_cluster = place_ends(jax.random.randint(key_of[3], (QUERIES,), 0, CPG), jax.random.fold_in(key_of[3], 1), 0, CPG - 1).astype(jnp.int32)
    member_cluster = jax.vmap(lambda own: jnp.searchsorted(jnp.cumsum(uneven_parts(own, CPG, GROUP_ROWS, GROUP_ROWS // 4, 2)), jnp.arange(GROUP_ROWS), side="right"))(jax.random.split(key_of[4], N_EX)).reshape((N_EX, GROUP_ROWS)).astype(jnp.int32)
    return {"embeddings": embeddings, "block_rows": block_rows, "owners": owners, "query_cluster": query_cluster, "member_cluster": member_cluster}


def unit_length(matrix):
    wide = matrix.astype(jnp.float32)
    squares = lax.optimization_barrier(jnp.sum(wide * wide, axis=1, keepdims=True))
    return (wide * lax.rsqrt(squares + 1e-06)).astype(jnp.bfloat16)

def reference(embeddings, block_rows, owners, query_cluster, member_cluster):
    members = unit_length(embeddings)
    queries = unit_length(block_rows)
    targets = owners[:, 0]
    most_rows = N_EX * N_REP * CAP

    def per_group(group):
        picked = jnp.nonzero(targets == group, size=most_rows, fill_value=QUERIES)[0].astype(jnp.int32)
        usable = picked < QUERIES
        clipped = jnp.minimum(picked, QUERIES - 1)
        chosen = queries[clipped]
        labels = query_cluster[clipped]
        local_members = lax.dynamic_slice_in_dim(members, (group * GROUP_ROWS).astype(jnp.int32), GROUP_ROWS, 0)
        local_labels = lax.dynamic_index_in_dim(member_cluster, group, 0, keepdims=False)
        cosines = jnp.dot(chosen, local_members.T, preferred_element_type=jnp.float32)
        same_cluster = usable[:, None] & (labels[:, None] == local_labels[None, :])
        scores = jnp.where(same_cluster, cosines, -1.0)
        return (lax.optimization_barrier(jnp.max(scores, axis=1)), picked, lax.optimization_barrier(jnp.max(scores, axis=0)))
    row_best, picked, column_best = lax.map(per_group, jnp.arange(N_EX, dtype=jnp.int32))
    query_max = jnp.full((QUERIES,), -1.0, jnp.float32).at[picked.reshape(-1)].max(row_best.reshape(-1), mode='drop')
    return (query_max, column_best.reshape(ROWS))
```

```python
import functools

import jax
import jax.numpy as jnp
import numpy as np
from jax import lax
from jax.experimental import pallas as pl
from jax.experimental.pallas import tpu as pltpu
from jax.sharding import PartitionSpec as P

MESH = pl.DeviceIdType.MESH
F32, BF16 = jnp.float32, jnp.bfloat16
EXACT = lax.Precision.HIGHEST
CAP = 12
PIECES = 6
TILE = 512


def layout_tables():
    spread = np.zeros((192, 192), np.float32)
    for r in range(192):
        a, k, s = r // 48, (r % 48) // CAP, r % CAP
        spread[r, k * 48 + a * CAP + s] = 1
    member_of = np.zeros((96, 8), np.float32)
    lane_of = np.zeros((96, 128), np.float32)
    for r in range(96):
        member_of[r, r // CAP] = 1
        lane_of[r, r % CAP] = 1
    return spread, spread.T.copy(), member_of, member_of.T.copy(), lane_of


def unit_length(block):
    wide = block.astype(F32)
    squares = jnp.sum(wide * wide, axis=1, keepdims=True)
    return (wide * lax.rsqrt(squares + 1e-06)).astype(BF16)


def dot(a, b, contract, precision=None):
    return lax.dot_general(a, b, ((contract[:1], contract[1:]), ((), ())), preferred_element_type=F32, precision=precision)


def kernel(
    emb_ref, rows_ref, owner_ref, qcl_ref, mcl_ref, spread_ref, gather_ref, memb_ref, membt_ref, lane_ref,
    qmax_ref, rmax_ref,
    out, arrive, lab_out, lab_in, q_own, q_par, lab_own, lab_par, ql_own, ql_par, m_own, m_par, ml_own, ml_par,
    rm_own, rm_par, b_send, b_got, c_own, c_par, c_got, ret_out, ret_in,
    load_sem, s_sem, r_sem, ls_sem, lr_sem, f_s, f_r, fl_s, fl_r, m_s, m_r, ml_s, ml_r, b_s, b_r, c_s, c_r, t_s, t_r,
):
    ex, rep = lax.axis_index("ex"), lax.axis_index("rep")
    core, z, y = ex % 2, (ex // 2) % 8, ex // 16
    near = rep + 1 - 2 * (rep % 2)
    m_mate = (1 - core) * near + core * (3 - rep)
    q_mate = (1 - core) * (3 - rep) + core * near

    def shift(j):
        i = j // 8
        dz = (i % 2) * ((i + 1) // 2) + (1 - i % 2) * ((8 - i // 2) % 8)
        return (j // 2) % 4, dz, j % 2

    def target(j):
        dy, dz, dc = shift(j)
        return ((((y + dy) % 4) * 8 + (z + dz) % 8) * 2 + (core + dc) % 2, rep)

    def origin(j):
        dy, dz, dc = shift(j)
        return ((((y + 4 - dy) % 4) * 8 + (z + 8 - dz) % 8) * 2 + (core + 2 - dc) % 2, rep)

    barrier = pltpu.get_barrier_semaphore()

    def greet(j, carry):
        pl.semaphore_signal(barrier, inc=1, device_id=target(j), device_id_type=MESH)
        return carry

    for mate in (m_mate, q_mate):
        pl.semaphore_signal(barrier, inc=1, device_id=(ex, mate), device_id_type=MESH)
    lax.fori_loop(1, 64, greet, 0)

    piece = m_own.shape[0] // PIECES
    load = pltpu.make_async_copy(emb_ref, m_own, load_sem)
    load.start()

    owners = owner_ref[...]
    dz = ((owners >> 1) - z) & 7
    order = jnp.where(dz == 0, 0, jnp.where(dz <= 4, 2 * dz - 1, 16 - 2 * dz))
    dest = order * 8 + (((owners >> 4) - y) & 3) * 2 + ((owners - core) & 1)
    count = owners.shape[1]
    is_dest = jnp.where(lax.broadcasted_iota(jnp.int32, (64, count), 0) == dest, 1.0, 0.0)
    earlier = jnp.where(
        lax.broadcasted_iota(jnp.int32, (count, count), 0) < lax.broadcasted_iota(jnp.int32, (count, count), 1), 1.0, 0.0
    ).astype(BF16)
    before = dot(is_dest.astype(BF16), earlier, (1, 0))
    rank = jnp.sum(is_dest * before, axis=0, keepdims=True).astype(jnp.int32)
    slot = dest * CAP + rank
    is_rank = jnp.where(lax.broadcasted_iota(jnp.int32, (128, count), 0) == rank, 1.0, 0.0)
    labels = (qcl_ref[...] + 1).astype(F32)
    lab_out[...] = dot((is_dest * labels).astype(BF16), is_rank.astype(BF16), (1, 1)).reshape(64, 1, 128)
    queries = unit_length(rows_ref[...])

    def place(g, carry):
        pick = jnp.where(lax.broadcasted_iota(jnp.int32, (48, count), 0) + g * 48 == slot, 1.0, 0.0).astype(BF16)
        rows = dot(pick, queries, (1, 0)).astype(BF16)
        stacked = jnp.concatenate([rows[:, k * 256 : (k + 1) * 256] for k in range(4)], axis=0)
        spread = dot(spread_ref[...], stacked, (1, 0)).astype(BF16)
        for a in range(4):
            out[g * 4 + a] = spread[a * 48 : (a + 1) * 48]
        return carry

    lax.fori_loop(0, 16, place, 0)

    load.wait()

    def normalize(p, carry):
        part = pl.ds(pl.multiple_of(p * 64, 64), 64)
        m_own[part, :] = unit_length(m_own[part, :])
        return carry

    lax.fori_loop(0, m_own.shape[0] // 64, normalize, 0)
    ml_own[...] = (mcl_ref[...] + 1).astype(F32)

    pl.semaphore_wait(barrier, 65)

    def member_copy(p):
        part = pl.ds(pl.multiple_of(p * piece, 64), piece)
        return pltpu.make_async_remote_copy(
            m_own.at[part], m_par.at[part], m_s.at[p], m_r.at[p], device_id=(ex, m_mate), device_id_type=MESH
        )

    def member_label_copy():
        return pltpu.make_async_remote_copy(ml_own, ml_par, ml_s, ml_r, device_id=(ex, m_mate), device_id_type=MESH)

    def send(j):
        return pltpu.make_async_remote_copy(
            out.at[j], arrive.at[j], s_sem.at[j // 8], r_sem.at[j // 8], device_id=target(j), device_id_type=MESH
        )

    def send_label(j):
        return pltpu.make_async_remote_copy(
            lab_out.at[j], lab_in.at[j], ls_sem.at[j // 8], lr_sem.at[j // 8], device_id=target(j), device_id_type=MESH
        )

    def forward(i):
        part = pl.ds(pl.multiple_of(i * 96, 96), 96)
        return pltpu.make_async_remote_copy(
            q_own.at[part], q_par.at[part], f_s.at[i], f_r.at[i], device_id=(ex, q_mate), device_id_type=MESH
        )

    def forward_label(i):
        part = pl.ds(pl.multiple_of(i * 8, 8), 8)
        return pltpu.make_async_remote_copy(
            lab_own.at[part], lab_par.at[part], fl_s.at[i], fl_r.at[i], device_id=(ex, q_mate), device_id_type=MESH
        )

    def start_members(p, carry):
        member_copy(p).start()
        return carry

    lax.fori_loop(0, PIECES, start_members, 0)
    member_label_copy().start()

    def start_send(j, carry):
        send(j).start()
        send_label(j).start()
        return carry

    lax.fori_loop(1, 64, start_send, 0)
    arrive[0] = out[0]
    lab_in[0] = lab_out[0]

    def settle(ref, sem, i, first):
        part = ref.at[pl.ds(i * 8 + first, 8 - first)]
        pltpu.make_async_copy(part, part, sem.at[i]).wait()

    def label_column(block):
        spread = dot(memb_ref[...], block.astype(BF16), (1, 0))
        return jnp.sum(spread * lane_ref[...], axis=1, keepdims=True)

    def take(i, first):
        settle(arrive, r_sem, i, first)
        settle(lab_in, lr_sem, i, first)
        for h in range(2):
            block = arrive[pl.ds(i * 8 + h * 4, 4)].reshape(192, 256)
            rows = dot(gather_ref[...], block, (1, 0)).astype(BF16)
            part = pl.ds(pl.multiple_of(i * 96 + h * 48, 48), 48)
            for k in range(4):
                q_own[part, k * 256 : (k + 1) * 256] = rows[k * 48 : (k + 1) * 48]
        lab = lab_in[pl.ds(i * 8, 8)].reshape(8, 128)
        lab_own[pl.ds(pl.multiple_of(i * 8, 8), 8), :] = lab
        forward(i).start()
        forward_label(i).start()
        ql_own[pl.ds(pl.multiple_of(i * 96, 96), 96), :] = label_column(lab)

    def take_next(i, carry):
        take(i, 0)
        return carry

    def take_forward(i, carry):
        forward(i).wait_recv()
        forward_label(i).wait_recv()
        lab = lab_par[pl.ds(pl.multiple_of(i * 8, 8), 8), :]
        ql_par[pl.ds(pl.multiple_of(i * 96, 96), 96), :] = label_column(lab)
        return carry

    c_own[...] = jnp.full(c_own.shape, -1.0, F32)
    c_par[...] = jnp.full(c_par.shape, -1.0, F32)
    rm_own[...] = jnp.full(rm_own.shape, -1.0, F32)
    rm_par[...] = jnp.full(rm_par.shape, -1.0, F32)

    def score(q_ref, ql_ref, row_ref, m_ref, ml_ref, col_ref, first, rows):
        labels = ql_ref[first : first + rows, :]
        part = q_ref[first : first + rows, :]

        def tile(t, best):
            at = pl.ds(pl.multiple_of(t * TILE, TILE), TILE)
            cosine = dot(part, m_ref[at, :], (1, 1))
            cosine = jnp.where(labels == ml_ref[:, at], cosine, -1.0)
            col_ref[:, at] = jnp.maximum(col_ref[:, at], jnp.max(cosine, axis=0, keepdims=True))
            for k in range(TILE // 128):
                best = jnp.maximum(best, cosine[:, k * 128 : (k + 1) * 128])
            return best

        best = lax.fori_loop(0, m_ref.shape[0] // TILE, tile, jnp.full((rows, 128), -1.0, F32))
        row_ref[first : first + rows, :] = jnp.maximum(row_ref[first : first + rows, :], jnp.max(best, axis=1, keepdims=True))

    def row_block(row_ref, i):
        column = row_ref[pl.ds(pl.multiple_of(i * 96, 96), 96), :] * lane_ref[...]
        return dot(membt_ref[...], column, (1, 0), EXACT)

    take(0, 1)
    lax.fori_loop(1, 4, take_next, 0)
    score(q_own, ql_own, rm_own, m_own, ml_own, c_own, 0, 384)
    lax.fori_loop(4, 8, take_next, 0)
    score(q_own, ql_own, rm_own, m_own, ml_own, c_own, 384, 384)
    lax.fori_loop(0, 4, take_forward, 0)
    score(q_par, ql_par, rm_par, m_own, ml_own, c_own, 0, 384)

    def take_members(p, carry):
        member_copy(p).wait_recv()
        return carry

    lax.fori_loop(0, PIECES, take_members, 0)
    member_label_copy().wait_recv()
    score(q_par, ql_par, rm_par, m_par, ml_par, c_par, 0, 384)

    def trade(i):
        part = pl.ds(pl.multiple_of(i * 8, 8), 8)
        return pltpu.make_async_remote_copy(
            b_send.at[part], b_got.at[part], b_s.at[i], b_r.at[i], device_id=(ex, q_mate), device_id_type=MESH
        )

    def start_trade(i, carry):
        b_send[pl.ds(pl.multiple_of(i * 8, 8), 8), :] = row_block(rm_par, i)
        trade(i).start()
        return carry

    lax.fori_loop(0, 4, start_trade, 0)
    score(q_own, ql_own, rm_own, m_par, ml_par, c_par, 0, 384)
    score(q_own, ql_own, rm_own, m_par, ml_par, c_par, 384, 384)
    lax.fori_loop(4, 8, take_forward, 0)
    score(q_par, ql_par, rm_par, m_own, ml_own, c_own, 384, 384)
    score(q_par, ql_par, rm_par, m_par, ml_par, c_par, 384, 384)
    lax.fori_loop(4, 8, start_trade, 0)
    columns = pltpu.make_async_remote_copy(c_par, c_got, c_s, c_r, device_id=(ex, m_mate), device_id_type=MESH)
    columns.start()

    def answer(j):
        return pltpu.make_async_remote_copy(ret_out.at[j], ret_in.at[j], t_s, t_r, device_id=origin(j), device_id_type=MESH)

    def merge(i, carry):
        trade(i).wait_recv()
        best = jnp.maximum(row_block(rm_own, i), b_got[pl.ds(pl.multiple_of(i * 8, 8), 8), :])
        ret_out[pl.ds(i * 8, 8)] = best.reshape(8, 1, 128)
        return carry

    lax.fori_loop(0, 8, merge, 0)

    def start_answer(j, carry):
        answer(j).start()
        return carry

    lax.fori_loop(1, 64, start_answer, 0)
    ret_in[0] = ret_out[0]
    columns.wait()
    rmax_ref[...] = jnp.maximum(c_own[...], c_got[...])

    for i in range(8):
        first = 1 if i == 0 else 0
        settle(out, s_sem, i, first)
        settle(lab_out, ls_sem, i, first)
        forward(i).wait_send()
        forward_label(i).wait_send()
        trade(i).wait_send()
    for p in range(PIECES):
        member_copy(p).wait_send()
    member_label_copy().wait_send()

    answers = ret_in.at[pl.ds(1, 63)]
    pltpu.make_async_copy(answers, answers, t_r).wait()
    sent = ret_out.at[pl.ds(1, 63)]
    pltpu.make_async_copy(sent, sent, t_s).wait()
    by_rank = dot(ret_in[...].reshape(64, 128), is_dest, (0, 0), EXACT)
    qmax_ref[...] = jnp.sum(by_rank * is_rank, axis=0, keepdims=True)


def shards(embeddings, block_rows, owners, query_cluster, member_cluster):
    members, width = embeddings.shape
    count = block_rows.shape[0]
    spread, gather, member_of, member_of_t, lane_of = layout_tables()
    vmem = pl.BlockSpec(memory_space=pltpu.VMEM)
    dma = pltpu.SemaphoreType.DMA
    query_max, resident_max = pl.pallas_call(
        kernel,
        out_shape=(jax.ShapeDtypeStruct((1, count), F32), jax.ShapeDtypeStruct((1, members), F32)),
        in_specs=[pl.BlockSpec(memory_space=pl.ANY)] + [vmem] * 9,
        out_specs=(vmem, vmem),
        scratch_shapes=[
            pltpu.VMEM((64, 48, 256), BF16),
            pltpu.VMEM((64, 48, 256), BF16),
            pltpu.VMEM((64, 1, 128), F32),
            pltpu.VMEM((64, 1, 128), F32),
            pltpu.VMEM((768, width), BF16),
            pltpu.VMEM((768, width), BF16),
            pltpu.VMEM((64, 128), F32),
            pltpu.VMEM((64, 128), F32),
            pltpu.VMEM((768, 1), F32),
            pltpu.VMEM((768, 1), F32),
            pltpu.VMEM((members, width), BF16),
            pltpu.VMEM((members, width), BF16),
            pltpu.VMEM((1, members), F32),
            pltpu.VMEM((1, members), F32),
            pltpu.VMEM((768, 1), F32),
            pltpu.VMEM((768, 1), F32),
            pltpu.VMEM((64, 128), F32),
            pltpu.VMEM((64, 128), F32),
            pltpu.VMEM((1, members), F32),
            pltpu.VMEM((1, members), F32),
            pltpu.VMEM((1, members), F32),
            pltpu.VMEM((64, 1, 128), F32),
            pltpu.VMEM((64, 1, 128), F32),
            dma,
            dma((8,)), dma((8,)), dma((8,)), dma((8,)),
            dma((8,)), dma((8,)), dma((8,)), dma((8,)),
            dma((PIECES,)), dma((PIECES,)), dma, dma,
            dma((8,)), dma((8,)), dma, dma, dma, dma,
        ],
        compiler_params=pltpu.CompilerParams(collective_id=0, has_side_effects=True, vmem_limit_bytes=48 << 20),
    )(
        embeddings,
        block_rows,
        owners.reshape(1, count),
        query_cluster.reshape(1, count),
        member_cluster,
        jnp.asarray(spread, BF16),
        jnp.asarray(gather, BF16),
        jnp.asarray(member_of, BF16),
        jnp.asarray(member_of_t, F32),
        jnp.asarray(lane_of, F32),
    )
    return query_max.reshape(count), resident_max.reshape(members)


def solution(mesh):
    placed = (
        P(("ex", "rep"), None),
        P(("ex", "rep"), None),
        P(("ex", "rep"), None),
        P(("ex", "rep")),
        P("ex", "rep"),
    )
    return jax.shard_map(
        shards,
        mesh=mesh,
        in_specs=placed,
        out_specs=(P(("ex", "rep")), P(("ex", "rep"))),
        check_vma=False,
    )
```

```python
import jax
import jax.numpy as jnp
from jax import lax
from jax.experimental import pallas as pl
from jax.experimental.pallas import tpu as pltpu
from jax.sharding import PartitionSpec as P

MESH = pl.DeviceIdType.MESH
F32, BF16 = jnp.float32, jnp.bfloat16
EXACT = lax.Precision.HIGHEST
CAP = 12
PIECES = 6


def unit_length(block):
    wide = block.astype(F32)
    squares = jnp.sum(wide * wide, axis=1, keepdims=True)
    return (wide * lax.rsqrt(squares + 1e-06)).astype(BF16)


def dot(a, b, contract, precision=None):
    return lax.dot_general(a, b, ((contract[:1], contract[1:]), ((), ())), preferred_element_type=F32, precision=precision)


def iota(shape, axis):
    return lax.broadcasted_iota(jnp.int32, shape, axis)


def one_hot(match):
    return jnp.where(match, 1.0, 0.0)


def spread_index(r):
    a = (r * 1366) >> 16
    rest = r - a * 48
    k = (rest * 5462) >> 16
    return k * 48 + a * CAP + rest - k * CAP


def kernel(
    emb_ref, rows_ref, owner_ref, qcl_ref, mcl_ref,
    qmax_ref, rmax_ref,
    rows, owner, qcl, mcl, spread, gather,
    out, arrive, lab_out, lab_in, q_own, q_par, ql_own, ql_par, m_own, m_par, ml_own, ml_par, mlb_own, mlb_par,
    r_own, r_par, r_got, c_own, c_par, c_send, c_got, ret_out, ret_in,
    load_sem, s_sem, r_sem, ls_sem, lr_sem, f_s, f_r, fl_s, fl_r, m_s, m_r, ml_s, ml_r, b_s, b_r, c_s, c_r, t_s, t_r,
):
    ex, rep = lax.axis_index("ex"), lax.axis_index("rep")
    core, z, y = ex % 2, (ex // 2) % 8, ex // 16
    near = rep + 1 - 2 * (rep % 2)
    m_mate = (1 - core) * near + core * (3 - rep)
    q_mate = (1 - core) * (3 - rep) + core * near

    def shift(j):
        i = j // 8
        dz = (i % 2) * ((i + 1) // 2) + (1 - i % 2) * ((8 - i // 2) % 8)
        return (j // 2) % 4, dz, j % 2

    def target(j):
        dy, dz, dc = shift(j)
        return ((((y + dy) % 4) * 8 + (z + dz) % 8) * 2 + (core + dc) % 2, rep)

    def origin(j):
        dy, dz, dc = shift(j)
        return ((((y + 4 - dy) % 4) * 8 + (z + 8 - dz) % 8) * 2 + (core + 2 - dc) % 2, rep)

    barrier = pltpu.get_barrier_semaphore()

    def greet(j, carry):
        pl.semaphore_signal(barrier, inc=1, device_id=target(j), device_id_type=MESH)
        return carry

    for mate in (m_mate, q_mate):
        pl.semaphore_signal(barrier, inc=1, device_id=(ex, mate), device_id_type=MESH)

    piece = m_own.shape[0] // PIECES
    small = [
        pltpu.make_async_copy(source, target_ref, load_sem.at[k])
        for k, (source, target_ref) in enumerate(
            ((owner_ref, owner), (qcl_ref, qcl), (mcl_ref, mcl), (rows_ref, rows))
        )
    ]
    for copy in small:
        copy.start()

    def load(p):
        part = pl.ds(p * piece, piece)
        return pltpu.make_async_copy(emb_ref.at[part], m_own.at[part], load_sem.at[4 + p])

    for p in range(PIECES):
        load(p).start()
    lax.fori_loop(1, 64, greet, 0)

    spread[...] = one_hot(iota((192, 192), 1) == spread_index(iota((192, 192), 0))).astype(BF16)
    gather[...] = one_hot(iota((192, 192), 0) == spread_index(iota((192, 192), 1))).astype(BF16)

    small[0].wait()
    small[1].wait()
    owners = owner[...]
    count = owners.shape[1]
    dz = ((owners >> 1) - z) & 7
    order = jnp.where(dz == 0, 0, jnp.where(dz <= 4, 2 * dz - 1, 16 - 2 * dz))
    dest = order * 8 + (((owners >> 4) - y) & 3) * 2 + ((owners - core) & 1)
    is_dest = one_hot(iota((64, count), 0) == dest)
    earlier = one_hot(iota((count, count), 0) < iota((count, count), 1)).astype(BF16)
    before = dot(is_dest.astype(BF16), earlier, (1, 0))
    rank = jnp.sum(is_dest * before, axis=0, keepdims=True).astype(jnp.int32)
    slot = dest * CAP + rank
    lane = (dest & 7) * CAP + rank
    is_lane = one_hot(iota((128, count), 0) == lane)
    labels = (jnp.concatenate([qcl[k : k + 1, :] for k in range(count // 128)], axis=1) + 1).astype(F32)
    lab_out[...] = dot((is_dest * labels).astype(BF16), is_lane.astype(BF16), (1, 1)).reshape(64, 1, 128)
    small[3].wait()
    rows[...] = unit_length(rows[...])

    def normalize(p):
        load(p).wait()

        def some(t, carry):
            part = pl.ds(pl.multiple_of(p * piece + t * 64, 64), 64)
            m_own[part, :] = unit_length(m_own[part, :])
            return carry

        lax.fori_loop(0, piece // 64, some, 0)

    def member_copy(p):
        part = pl.ds(p * piece, piece)
        return pltpu.make_async_remote_copy(
            m_own.at[part], m_par.at[part], m_s.at[p], m_r.at[p], device_id=(ex, m_mate), device_id_type=MESH
        )

    def member_label_copy():
        return pltpu.make_async_remote_copy(ml_own, ml_par, ml_s, ml_r, device_id=(ex, m_mate), device_id_type=MESH)

    def send(j):
        return pltpu.make_async_remote_copy(
            out.at[j], arrive.at[j], s_sem.at[j // 8], r_sem.at[j // 8], device_id=target(j), device_id_type=MESH
        )

    def send_label(j):
        return pltpu.make_async_remote_copy(
            lab_out.at[j], lab_in.at[j], ls_sem.at[j // 8], lr_sem.at[j // 8], device_id=target(j), device_id_type=MESH
        )

    def forward(i):
        part = pl.ds(pl.multiple_of(i * 96, 96), 96)
        return pltpu.make_async_remote_copy(
            q_own.at[part], q_par.at[part], f_s.at[i], f_r.at[i], device_id=(ex, q_mate), device_id_type=MESH
        )

    def forward_labels(h):
        return pltpu.make_async_remote_copy(
            ql_own.at[h], ql_par.at[h], fl_s.at[h], fl_r.at[h], device_id=(ex, q_mate), device_id_type=MESH
        )

    small[2].wait()
    ml_own[...] = (mcl[...] + 1).astype(F32)
    normalize(0)
    pl.semaphore_wait(barrier, 65)
    member_label_copy().start()
    member_copy(0).start()

    def place(g):
        pick = one_hot(iota((192, count), 0) + g * 192 == slot).astype(BF16)
        placed = dot(pick, rows[...], (1, 0)).astype(BF16)
        for q in range(4):
            four = placed[q * 48 : (q + 1) * 48]
            stacked = jnp.concatenate([four[:, k * 256 : (k + 1) * 256] for k in range(4)], axis=0)
            laid = dot(spread[...], stacked, (1, 0)).astype(BF16)
            for a in range(4):
                out[g * 16 + q * 4 + a] = laid[a * 48 : (a + 1) * 48]

    def start_send(j, carry):
        send(j).start()
        send_label(j).start()
        return carry

    def place_next(g, carry):
        place(g)
        lax.fori_loop(g * 16, g * 16 + 16, start_send, 0)
        return carry

    place(0)
    lax.fori_loop(1, 16, start_send, 0)
    lax.fori_loop(1, 4, place_next, 0)
    arrive[0] = out[0]
    lab_in[0] = lab_out[0]
    for p in range(1, PIECES):
        normalize(p)
        member_copy(p).start()

    def widen(row_ref, wide_ref):
        for b in range(row_ref.shape[1] // 128):
            part = jnp.broadcast_to(row_ref[:, b * 128 : (b + 1) * 128], (128, 128))
            wide_ref[b * 128 : (b + 1) * 128, :] = part.T

    widen(ml_own, mlb_own)
    c_own[...] = jnp.full(c_own.shape, -1.0, F32)
    c_par[...] = jnp.full(c_par.shape, -1.0, F32)
    r_own[...] = jnp.full(r_own.shape, -1.0, F32)
    r_par[...] = jnp.full(r_par.shape, -1.0, F32)

    def settle(ref, sem, i, first):
        part = ref.at[pl.ds(i * 8 + first, 8 - first)]
        pltpu.make_async_copy(part, part, sem.at[i]).wait()

    def take(i, first):
        settle(arrive, r_sem, i, first)
        for h in range(2):
            block = arrive[pl.ds(i * 8 + h * 4, 4)].reshape(192, 256)
            back = dot(gather[...], block, (1, 0)).astype(BF16)
            part = pl.ds(pl.multiple_of(i * 96 + h * 48, 48), 48)
            for k in range(4):
                q_own[part, k * 256 : (k + 1) * 256] = back[k * 48 : (k + 1) * 48]
        forward(i).start()

    def take_next(i, carry):
        take(i, 0)
        return carry

    def take_labels(h):
        parts = []
        for i in range(h * 4, h * 4 + 4):
            settle(lab_in, lr_sem, i, 1 if i == 0 else 0)
            parts.append(jnp.sum(lab_in[i * 8 : i * 8 + 8], axis=0)[:, :96])
        ql_own[h] = jnp.concatenate(parts, axis=1)
        forward_labels(h).start()

    def take_forward(i, carry):
        forward(i).wait_recv()
        return carry

    def score(q_ref, ql_ref, row_ref, halves, m_ref, mlb_ref, col_ref, first, tiles):
        width = 384 * len(halves)
        start = 384 * halves[0]
        label_row = jnp.concatenate([ql_ref[h] for h in halves], axis=1)

        def tile(t, best):
            at = pl.ds(pl.multiple_of(first + t * 256, 256), 256)
            cosine = dot(m_ref[at, :], q_ref[start : start + width, :], (1, 1))
            wide = mlb_ref[at, :]
            column = col_ref[at, :]
            parts = []
            for k in range(width // 128):
                here = slice(k * 128, (k + 1) * 128)
                value = jnp.where(wide == label_row[:, here], cosine[:, here], -1.0)
                column = jnp.maximum(column, value)
                parts.append(jnp.max(value.reshape(32, 8, 128), axis=0))
            col_ref[at, :] = column
            return jnp.maximum(best, jnp.concatenate(parts, axis=1))

        best = lax.fori_loop(0, tiles, tile, jnp.full((8, width), -1.0, F32))
        there = slice(start, start + width)
        row_ref[:, there] = jnp.maximum(row_ref[:, there], jnp.max(best, axis=0, keepdims=True))

    own = m_own.shape[0] // 256
    take(0, 1)
    lax.fori_loop(1, 4, take_next, 0)
    take_labels(0)
    score(q_own, ql_own, r_own, (0,), m_own, mlb_own, c_own, 0, own)
    lax.fori_loop(4, 8, take_next, 0)
    take_labels(1)
    score(q_own, ql_own, r_own, (1,), m_own, mlb_own, c_own, 0, own)
    lax.fori_loop(0, 4, take_forward, 0)
    forward_labels(0).wait_recv()
    score(q_par, ql_par, r_par, (0,), m_own, mlb_own, c_own, 0, own)
    member_label_copy().wait_recv()
    widen(ml_par, mlb_par)
    lax.fori_loop(4, 8, take_forward, 0)
    forward_labels(1).wait_recv()
    score(q_par, ql_par, r_par, (1,), m_own, mlb_own, c_own, 0, own)
    for p in range(PIECES):
        member_copy(p).wait_recv()
        score(q_par, ql_par, r_par, (0, 1), m_par, mlb_par, c_par, p * piece, piece // 256)
        if p == PIECES - 1:
            trade = pltpu.make_async_remote_copy(r_par, r_got, b_s, b_r, device_id=(ex, q_mate), device_id_type=MESH)
            trade.start()
        score(q_own, ql_own, r_own, (0, 1), m_par, mlb_par, c_par, p * piece, piece // 256)

    def columns_of(col_ref, b):
        return jnp.max(col_ref[b * 128 : (b + 1) * 128, :].T, axis=0, keepdims=True)

    trade.wait_recv()
    merged = jnp.maximum(r_own[...], r_got[...])
    for i in range(8):
        ret_out[i] = jnp.concatenate([merged[:, i * 96 : (i + 1) * 96], jnp.zeros((1, 32), F32)], axis=1)

    def answer(j):
        return pltpu.make_async_remote_copy(
            ret_out.at[j // 8], ret_in.at[j], t_s, t_r, device_id=origin(j), device_id_type=MESH
        )

    def start_answer(j, carry):
        answer(j).start()
        return carry

    lax.fori_loop(1, 64, start_answer, 0)
    ret_in[0] = ret_out[0]
    blocks = c_par.shape[0] // 128
    for b in range(blocks):
        c_send[b : b + 1, :] = columns_of(c_par, b)
    columns = pltpu.make_async_remote_copy(c_send, c_got, c_s, c_r, device_id=(ex, m_mate), device_id_type=MESH)
    columns.start()
    for b in range(blocks):
        rmax_ref[b : b + 1, :] = columns_of(c_own, b)

    for i in range(8):
        first = 1 if i == 0 else 0
        settle(out, s_sem, i, first)
        settle(lab_out, ls_sem, i, first)
        forward(i).wait_send()
    for h in range(2):
        forward_labels(h).wait_send()
    for p in range(PIECES):
        member_copy(p).wait_send()
    member_label_copy().wait_send()
    trade.wait_send()

    answers = ret_in.at[pl.ds(1, 63)]
    pltpu.make_async_copy(answers, answers, t_s).wait()
    pltpu.make_async_copy(answers, answers, t_r).wait()
    by_lane = dot(ret_in[...].reshape(64, 128), is_dest, (0, 0), EXACT)
    result = jnp.sum(by_lane * is_lane, axis=0, keepdims=True)
    for k in range(count // 128):
        qmax_ref[k : k + 1, :] = result[:, k * 128 : (k + 1) * 128]
    columns.wait()
    rmax_ref[...] = jnp.maximum(rmax_ref[...], c_got[...])


def shards(embeddings, block_rows, owners, query_cluster, member_cluster):
    members, width = embeddings.shape
    count = block_rows.shape[0]
    vmem = pl.BlockSpec(memory_space=pltpu.VMEM)
    dma = pltpu.SemaphoreType.DMA
    v = pltpu.VMEM
    query_max, resident_max = pl.pallas_call(
        kernel,
        out_shape=(jax.ShapeDtypeStruct((count // 128, 128), F32), jax.ShapeDtypeStruct((members // 128, 128), F32)),
        in_specs=[pl.BlockSpec(memory_space=pl.ANY)] * 5,
        out_specs=(vmem, vmem),
        scratch_shapes=[
            v((count, width), BF16), v((1, count), jnp.int32), v((count // 128, 128), jnp.int32), v((1, members), jnp.int32),
            v((192, 192), BF16), v((192, 192), BF16),
            v((64, 48, 256), BF16), v((64, 48, 256), BF16), v((64, 1, 128), F32), v((64, 1, 128), F32),
            v((768, width), BF16), v((768, width), BF16), v((2, 1, 384), F32), v((2, 1, 384), F32),
            v((members, width), BF16), v((members, width), BF16), v((1, members), F32), v((1, members), F32),
            v((members, 128), F32), v((members, 128), F32),
            v((1, 768), F32), v((1, 768), F32), v((1, 768), F32),
            v((members, 128), F32), v((members, 128), F32), v((members // 128, 128), F32), v((members // 128, 128), F32),
            v((8, 1, 128), F32), v((64, 1, 128), F32),
            dma((4 + PIECES,)),
            dma((8,)), dma((8,)), dma((8,)), dma((8,)),
            dma((8,)), dma((8,)), dma((2,)), dma((2,)),
            dma((PIECES,)), dma((PIECES,)), dma, dma,
            dma, dma, dma, dma, dma, dma,
        ],
        compiler_params=pltpu.CompilerParams(collective_id=0, has_side_effects=True, vmem_limit_bytes=56 << 20),
    )(
        embeddings,
        block_rows,
        owners.reshape(1, count),
        query_cluster.reshape(count // 128, 128),
        member_cluster,
    )
    return query_max.reshape(count), resident_max.reshape(members)


def solution(mesh):
    placed = (
        P(("ex", "rep"), None),
        P(("ex", "rep"), None),
        P(("ex", "rep"), None),
        P(("ex", "rep")),
        P("ex", "rep"),
    )
    return jax.shard_map(
        shards,
        mesh=mesh,
        in_specs=placed,
        out_specs=(P(("ex", "rep")), P(("ex", "rep"))),
        check_vma=False,
    )
```

```python
import jax
import jax.numpy as jnp
from jax import lax
from jax.experimental import pallas as pl
from jax.experimental.pallas import tpu as pltpu
from jax.sharding import PartitionSpec as P

MESH = pl.DeviceIdType.MESH
F32, BF16 = jnp.float32, jnp.bfloat16
EXACT = lax.Precision.HIGHEST
CAP = 12
PIECES = 6


def unit_length(block):
    wide = block.astype(F32)
    squares = jnp.sum(wide * wide, axis=1, keepdims=True)
    return (wide * lax.rsqrt(squares + 1e-06)).astype(BF16)


def dot(a, b, contract, precision=None):
    return lax.dot_general(a, b, ((contract[:1], contract[1:]), ((), ())), preferred_element_type=F32, precision=precision)


def iota(shape, axis):
    return lax.broadcasted_iota(jnp.int32, shape, axis)


def one_hot(match):
    return jnp.where(match, 1.0, 0.0)


def spread_index(r):
    a = (r * 1366) >> 16
    rest = r - a * 48
    k = (rest * 5462) >> 16
    return k * 48 + a * CAP + rest - k * CAP


def kernel(
    emb_ref, rows_ref, owner_ref, qcl_ref, mcl_ref,
    qmax_ref, rmax_ref,
    rows, owner, qcl, mcl, spread, gather,
    out, arrive, lab_out, lab_in, q_own, q_par, ql_own, ql_par, m_own, m_par, ml_own, ml_par, mlb_own, mlb_par,
    r_own, r_par, r_got, c_own, c_par, c_send, c_got, ret_out, ret_mid, ret_in,
    load_sem, s_sem, r_sem, ls_sem, lr_sem, f_s, f_r, fl_s, fl_r, m_s, m_r, ml_s, ml_r, b_s, b_r, c_s, c_r, tz_s, tz_r, t_s, t_r,
):
    ex, rep = lax.axis_index("ex"), lax.axis_index("rep")
    core, z, y = lax.rem(ex, 2), lax.rem(lax.div(ex, 2), 8), lax.div(ex, 16)
    near = rep + 1 - 2 * lax.rem(rep, 2)
    m_mate = (1 - core) * near + core * (3 - rep)
    q_mate = (1 - core) * (3 - rep) + core * near

    def place_at(dy, dz, dc):
        return ((lax.rem(y + dy, 4) * 8 + lax.rem(z + dz, 8)) * 2 + lax.rem(core + dc, 2), rep)

    def shift(j):
        if isinstance(j, int):
            i = j // 8
            return (j // 2) % 4, ((i + 1) // 2 if i % 2 else (8 - i // 2) % 8), j % 2
        i = lax.div(j, 8)
        odd = lax.rem(i, 2)
        half = lax.div(i + 1, 2)
        return lax.rem(lax.div(j, 2), 4), odd * half + (1 - odd) * lax.rem(8 - half, 8), lax.rem(j, 2)

    def target(j):
        return place_at(*shift(j))

    barrier = pltpu.get_barrier_semaphore()

    def greet(j, carry):
        pl.semaphore_signal(barrier, inc=1, device_id=target(j), device_id_type=MESH)
        return carry

    for mate in (m_mate, q_mate):
        pl.semaphore_signal(barrier, inc=1, device_id=(ex, mate), device_id_type=MESH)

    piece = m_own.shape[0] // PIECES
    small = [
        pltpu.make_async_copy(source, target_ref, load_sem.at[k])
        for k, (source, target_ref) in enumerate(
            ((owner_ref, owner), (qcl_ref, qcl), (mcl_ref, mcl), (rows_ref, rows))
        )
    ]
    for copy in small:
        copy.start()

    def load(p):
        part = pl.ds(p * piece, piece)
        return pltpu.make_async_copy(emb_ref.at[part], m_own.at[part], load_sem.at[4 + p])

    for p in range(PIECES):
        load(p).start()
    lax.fori_loop(1, 64, greet, 0)

    spread[...] = one_hot(iota((192, 192), 1) == spread_index(iota((192, 192), 0))).astype(BF16)
    gather[...] = one_hot(iota((192, 192), 0) == spread_index(iota((192, 192), 1))).astype(BF16)

    small[0].wait()
    small[1].wait()
    owners = owner[...]
    count = owners.shape[1]
    dz = ((owners >> 1) - z) & 7
    order = jnp.where(dz == 0, 0, jnp.where(dz <= 4, 2 * dz - 1, 16 - 2 * dz))
    dest = order * 8 + (((owners >> 4) - y) & 3) * 2 + ((owners - core) & 1)
    is_dest = one_hot(iota((64, count), 0) == dest)
    earlier = one_hot(iota((count, count), 0) < iota((count, count), 1)).astype(BF16)
    before = dot(is_dest.astype(BF16), earlier, (1, 0))
    rank = jnp.sum(is_dest * before, axis=0, keepdims=True).astype(jnp.int32)
    slot = dest * CAP + rank
    lane = (dest & 7) * CAP + rank
    is_lane = one_hot(iota((128, count), 0) == lane)
    labels = (jnp.concatenate([qcl[k : k + 1, :] for k in range(count // 128)], axis=1) + 1).astype(F32)
    lab_out[...] = dot((is_dest * labels).astype(BF16), is_lane.astype(BF16), (1, 1)).reshape(64, 1, 128)
    small[3].wait()
    rows[...] = unit_length(rows[...])

    def normalize(p):
        load(p).wait()

        def some(t, carry):
            part = pl.ds(pl.multiple_of(p * piece + t * 64, 64), 64)
            m_own[part, :] = unit_length(m_own[part, :])
            return carry

        lax.fori_loop(0, piece // 64, some, 0)

    def member_copy(p):
        part = pl.ds(p * piece, piece)
        return pltpu.make_async_remote_copy(
            m_own.at[part], m_par.at[part], m_s.at[p], m_r.at[p], device_id=(ex, m_mate), device_id_type=MESH
        )

    def member_label_copy():
        return pltpu.make_async_remote_copy(ml_own, ml_par, ml_s, ml_r, device_id=(ex, m_mate), device_id_type=MESH)

    def send(j):
        return pltpu.make_async_remote_copy(
            out.at[j], arrive.at[j], s_sem.at[lax.div(j, 8)], r_sem.at[lax.div(j, 8)], device_id=target(j), device_id_type=MESH
        )

    def send_label(j):
        return pltpu.make_async_remote_copy(
            lab_out.at[j], lab_in.at[j], ls_sem.at[lax.div(j, 8)], lr_sem.at[lax.div(j, 8)], device_id=target(j), device_id_type=MESH
        )

    def forward(i):
        part = pl.ds(pl.multiple_of(i * 96, 96), 96)
        return pltpu.make_async_remote_copy(
            q_own.at[part], q_par.at[part], f_s.at[i], f_r.at[i], device_id=(ex, q_mate), device_id_type=MESH
        )

    def forward_labels(h):
        return pltpu.make_async_remote_copy(
            ql_own.at[h], ql_par.at[h], fl_s.at[h], fl_r.at[h], device_id=(ex, q_mate), device_id_type=MESH
        )

    small[2].wait()
    ml_own[...] = (mcl[...] + 1).astype(F32)
    normalize(0)
    pl.semaphore_wait(barrier, 65)
    member_label_copy().start()
    member_copy(0).start()

    def place(g):
        pick = one_hot(iota((192, count), 0) + g * 192 == slot).astype(BF16)
        placed = dot(pick, rows[...], (1, 0)).astype(BF16)
        for q in range(4):
            four = placed[q * 48 : (q + 1) * 48]
            stacked = jnp.concatenate([four[:, k * 256 : (k + 1) * 256] for k in range(4)], axis=0)
            laid = dot(spread[...], stacked, (1, 0)).astype(BF16)
            for a in range(4):
                out[g * 16 + q * 4 + a] = laid[a * 48 : (a + 1) * 48]

    def start_send(j, carry):
        send(j).start()
        send_label(j).start()
        return carry

    def place_next(g, carry):
        place(g)
        lax.fori_loop(g * 16, g * 16 + 16, start_send, 0)
        return carry

    place(0)
    lax.fori_loop(1, 16, start_send, 0)
    lax.fori_loop(1, 4, place_next, 0)
    arrive[0] = out[0]
    lab_in[0] = lab_out[0]
    for p in range(1, PIECES):
        normalize(p)
        member_copy(p).start()

    def widen(row_ref, wide_ref):
        for b in range(row_ref.shape[1] // 128):
            part = jnp.broadcast_to(row_ref[:, b * 128 : (b + 1) * 128], (128, 128))
            wide_ref[b * 128 : (b + 1) * 128, :] = part.T

    widen(ml_own, mlb_own)
    c_own[...] = jnp.full(c_own.shape, -1.0, F32)
    c_par[...] = jnp.full(c_par.shape, -1.0, F32)
    r_own[...] = jnp.full(r_own.shape, -1.0, F32)
    r_par[...] = jnp.full(r_par.shape, -1.0, F32)

    def settle(ref, sem, i, first):
        part = ref.at[pl.ds(i * 8 + first, 8 - first)]
        pltpu.make_async_copy(part, part, sem.at[i]).wait()

    def take(i, first):
        settle(arrive, r_sem, i, first)
        for h in range(2):
            block = arrive[pl.ds(i * 8 + h * 4, 4)].reshape(192, 256)
            back = dot(gather[...], block, (1, 0)).astype(BF16)
            part = pl.ds(pl.multiple_of(i * 96 + h * 48, 48), 48)
            for k in range(4):
                q_own[part, k * 256 : (k + 1) * 256] = back[k * 48 : (k + 1) * 48]
        forward(i).start()

    def take_next(i, carry):
        take(i, 0)
        return carry


    def take_labels(h):
        parts = []
        for i in range(h * 4, h * 4 + 4):
            settle(lab_in, lr_sem, i, 1 if i == 0 else 0)
            parts.append(jnp.sum(lab_in[i * 8 : i * 8 + 8], axis=0)[:, :96])
        ql_own[h] = jnp.concatenate(parts, axis=1)
        forward_labels(h).start()

    def take_forward(i, carry):
        forward(i).wait_recv()
        return carry

    def score(q_ref, ql_ref, row_ref, chunks, m_ref, mlb_ref, col_ref, first, rows):
        width, start = 96 * len(chunks), 96 * chunks[0]
        step = min(rows, 512)
        label_row = jnp.concatenate([ql_ref[h] for h in range(chunks[0] // 4, chunks[-1] // 4 + 1)], axis=1)

        def tile(t, best):
            at = pl.ds(pl.multiple_of(first + t * step, 256), step)
            cosine = dot(m_ref[at, :], q_ref[start : start + width, :], (1, 1))
            wide = mlb_ref[at, :]
            parts = []
            for k in range(0, width, 128):
                n = min(128, width - k)
                value = jnp.where(wide[:, :n] == label_row[:, k : k + n], cosine[:, k : k + n], -1.0)
                col_ref[at, :n] = jnp.maximum(col_ref[at, :n], value)
                parts.append(jnp.max(value.reshape(step // 8, 8, n), axis=0))
            return jnp.maximum(best, jnp.concatenate(parts, axis=1))

        best = lax.fori_loop(0, rows // step, tile, jnp.full((8, width), -1.0, F32))
        best = jnp.max(best, axis=0, keepdims=True)
        for k, i in enumerate(chunks):
            row_ref[i, :, :96] = jnp.maximum(row_ref[i, :, :96], best[:, k * 96 : (k + 1) * 96])

    members = m_own.shape[0]
    whole, low, high = range(8), range(4), range(4, 8)

    def score_own(q_ref, ql_ref, row_ref, chunks):
        score(q_ref, ql_ref, row_ref, chunks, m_own, mlb_own, c_own, 0, members)

    def score_pieces(q_ref, ql_ref, row_ref, chunks, first, last):
        score(q_ref, ql_ref, row_ref, chunks, m_par, mlb_par, c_par, first * piece, (last - first) * piece)

    def members_in(first, last):
        for p in range(first, last):
            member_copy(p).wait_recv()

    take(0, 1)
    lax.fori_loop(1, 4, take_next, 0)
    take_labels(0)
    score_own(q_own, ql_own, r_own, low)
    take(4, 0)
    member_label_copy().wait_recv()
    widen(ml_par, mlb_par)
    forward_labels(0).wait_recv()
    take(5, 0)
    lax.fori_loop(0, 4, take_forward, 0)
    score_own(q_par, ql_par, r_par, low)
    take(6, 0)
    members_in(0, 2)
    score_pieces(q_own, ql_own, r_own, low, 0, 2)
    score_pieces(q_par, ql_par, r_par, low, 0, 2)
    take(7, 0)
    take_labels(1)
    score_own(q_own, ql_own, r_own, high)
    score_pieces(q_own, ql_own, r_own, high, 0, 2)
    members_in(2, 4)
    score_pieces(q_own, ql_own, r_own, whole, 2, 4)
    score_pieces(q_par, ql_par, r_par, low, 2, 4)
    forward_labels(1).wait_recv()
    lax.fori_loop(4, 8, take_forward, 0)
    score_own(q_par, ql_par, r_par, high)
    score_pieces(q_par, ql_par, r_par, high, 0, 4)
    for p in range(4, PIECES):
        members_in(p, p + 1)
        score_pieces(q_par, ql_par, r_par, whole, p, p + 1)
        if p == PIECES - 1:
            trade = pltpu.make_async_remote_copy(r_par, r_got, b_s, b_r, device_id=(ex, q_mate), device_id_type=MESH)
            trade.start()
        score_pieces(q_own, ql_own, r_own, whole, p, p + 1)

    def columns_of(col_ref, b):
        return jnp.max(col_ref[b * 128 : (b + 1) * 128, :].T, axis=0, keepdims=True)

    def answer_z(i):
        return pltpu.make_async_remote_copy(
            ret_out.at[i], ret_mid.at[i], tz_s.at[i], tz_r, device_id=place_at(0, 8 - shift(8 * i)[1], 0), device_id_type=MESH
        )

    def answer_y(k):
        return pltpu.make_async_remote_copy(
            ret_mid, ret_in.at[k], t_s.at[k], t_r, device_id=place_at(4 - k // 2, 0, 2 - k % 2), device_id_type=MESH
        )

    trade.wait_recv()
    for i in range(1, 8):
        ret_out[i] = jnp.maximum(r_own[i], r_got[i])
        answer_z(i).start()
    ret_mid[0] = jnp.maximum(r_own[0], r_got[0])
    blocks = members // 128
    for b in range(blocks):
        c_send[:, b * 128 : (b + 1) * 128] = columns_of(c_par, b)
    columns = pltpu.make_async_remote_copy(c_send, c_got, c_s, c_r, device_id=(ex, m_mate), device_id_type=MESH)
    columns.start()
    far = ret_mid.at[pl.ds(1, 7)]
    pltpu.make_async_copy(far, far, tz_r).wait()
    for k in range(1, 8):
        answer_y(k).start()
    ret_in[0] = ret_mid[...]
    for b in range(blocks):
        rmax_ref[:, b * 128 : (b + 1) * 128] = columns_of(c_own, b)

    for i in range(8):
        first = 1 if i == 0 else 0
        settle(out, s_sem, i, first)
        settle(lab_out, ls_sem, i, first)
        forward(i).wait_send()
    for h in range(2):
        forward_labels(h).wait_send()
    member_label_copy().wait_send()
    for p in range(PIECES):
        member_copy(p).wait_send()
    trade.wait_send()

    for k in range(1, 8):
        answer_z(k).wait_send()
        answer_y(k).wait_send()
    answers = ret_in.at[pl.ds(1, 7)]
    pltpu.make_async_copy(answers, answers, t_r).wait()
    by_row = one_hot(iota((64, count), 0) == (dest & 7) * 8 + (dest >> 3))
    by_lane = dot(ret_in[...].reshape(64, 128), by_row, (0, 0), EXACT)
    qmax_ref[...] = jnp.sum(by_lane * is_lane, axis=0, keepdims=True)
    columns.wait()
    rmax_ref[...] = jnp.maximum(rmax_ref[...], c_got[...])


def shards(embeddings, block_rows, owners, query_cluster, member_cluster):
    members, width = embeddings.shape
    count = block_rows.shape[0]
    vmem = pl.BlockSpec(memory_space=pltpu.VMEM)
    dma = pltpu.SemaphoreType.DMA
    v = pltpu.VMEM
    query_max, resident_max = pl.pallas_call(
        kernel,
        out_shape=(jax.ShapeDtypeStruct((1, count), F32), jax.ShapeDtypeStruct((1, members), F32)),
        in_specs=[pl.BlockSpec(memory_space=pl.ANY)] * 5,
        out_specs=(vmem, vmem),
        scratch_shapes=[
            v((count, width), BF16), v((1, count), jnp.int32), v((count // 128, 128), jnp.int32), v((1, members), jnp.int32),
            v((192, 192), BF16), v((192, 192), BF16),
            v((64, 48, 256), BF16), v((64, 48, 256), BF16), v((64, 1, 128), F32), v((64, 1, 128), F32),
            v((768, width), BF16), v((768, width), BF16), v((2, 1, 384), F32), v((2, 1, 384), F32),
            v((members, width), BF16), v((members, width), BF16), v((1, members), F32), v((1, members), F32),
            v((members, 128), F32), v((members, 128), F32),
            v((8, 1, 128), F32), v((8, 1, 128), F32), v((8, 1, 128), F32),
            v((members, 128), F32), v((members, 128), F32), v((1, members), F32), v((1, members), F32),
            v((8, 1, 128), F32), v((8, 1, 128), F32), v((8, 8, 1, 128), F32),
            dma((4 + PIECES,)),
            dma((8,)), dma((8,)), dma((8,)), dma((8,)),
            dma((8,)), dma((8,)), dma((2,)), dma((2,)),
            dma((PIECES,)), dma((PIECES,)), dma, dma,
            dma, dma, dma, dma, dma((8,)), dma, dma((8,)), dma,
        ],
        compiler_params=pltpu.CompilerParams(collective_id=0, has_side_effects=True, vmem_limit_bytes=56 << 20),
    )(
        embeddings,
        block_rows,
        owners.reshape(1, count),
        query_cluster.reshape(count // 128, 128),
        member_cluster,
    )
    return query_max.reshape(count), resident_max.reshape(members)


def solution(mesh):
    placed = (
        P(("ex", "rep"), None),
        P(("ex", "rep"), None),
        P(("ex", "rep"), None),
        P(("ex", "rep")),
        P("ex", "rep"),
    )
    return jax.shard_map(
        shards,
        mesh=mesh,
        in_specs=placed,
        out_specs=(P(("ex", "rep")), P(("ex", "rep"))),
        check_vma=False,
    )
```

```python
import jax
import jax.numpy as jnp
from jax import lax
from jax.experimental import pallas as pl
from jax.experimental.pallas import tpu as pltpu
from jax.sharding import PartitionSpec as P

MESH = pl.DeviceIdType.MESH
F32, BF16 = jnp.float32, jnp.bfloat16
EXACT = lax.Precision.HIGHEST
CAP = 12
PIECES = 6


def unit_length(block):
    wide = block.astype(F32)
    squares = jnp.sum(wide * wide, axis=1, keepdims=True)
    return (wide * lax.rsqrt(squares + 1e-06)).astype(BF16)


def dot(a, b, contract, precision=None):
    return lax.dot_general(a, b, ((contract[:1], contract[1:]), ((), ())), preferred_element_type=F32, precision=precision)


def iota(shape, axis):
    return lax.broadcasted_iota(jnp.int32, shape, axis)


def one_hot(match):
    return jnp.where(match, 1.0, 0.0)


def spread_index(r):
    a = (r * 1366) >> 16
    rest = r - a * 48
    k = (rest * 5462) >> 16
    return k * 48 + a * CAP + rest - k * CAP


def kernel(
    emb_ref, rows_ref, owner_ref, qcl_ref, mcl_ref,
    qmax_ref, rmax_ref,
    rows, owner, qcl, mcl, spread, gather,
    out, arrive, lab_out, lab_in, q_own, q_par, ql_own, ql_par, m_own, m_par, ml_own, ml_par, mlb_own, mlb_par,
    r_own, r_par, r_got, c_own, c_par, c_send, c_got, ret_out, ret_mid, ret_in,
    load_sem, s_sem, r_sem, ls_sem, lr_sem, f_s, f_r, fl_s, fl_r, m_s, m_r, ml_s, ml_r, b_s, b_r, c_s, c_r, tz_s, tz_r, t_s, t_r,
):
    ex, rep = lax.axis_index("ex"), lax.axis_index("rep")
    core, z, y = lax.rem(ex, 2), lax.rem(lax.div(ex, 2), 8), lax.div(ex, 16)
    near = rep + 1 - 2 * lax.rem(rep, 2)
    m_mate = (1 - core) * near + core * (3 - rep)
    q_mate = (1 - core) * (3 - rep) + core * near

    def place_at(dy, dz, dc):
        return ((lax.rem(y + dy, 4) * 8 + lax.rem(z + dz, 8)) * 2 + lax.rem(core + dc, 2), rep)

    def shift(j):
        if isinstance(j, int):
            i = j // 8
            return (j // 2) % 4, ((i + 1) // 2 if i % 2 else (8 - i // 2) % 8), j % 2
        i = lax.div(j, 8)
        odd = lax.rem(i, 2)
        half = lax.div(i + 1, 2)
        return lax.rem(lax.div(j, 2), 4), odd * half + (1 - odd) * lax.rem(8 - half, 8), lax.rem(j, 2)

    def target(j):
        return place_at(*shift(j))

    barrier = pltpu.get_barrier_semaphore()

    def greet(j, carry):
        pl.semaphore_signal(barrier, inc=1, device_id=target(j), device_id_type=MESH)
        return carry

    for mate in (m_mate, q_mate):
        pl.semaphore_signal(barrier, inc=1, device_id=(ex, mate), device_id_type=MESH)

    piece = m_own.shape[0] // PIECES
    small = [
        pltpu.make_async_copy(source, target_ref, load_sem.at[k])
        for k, (source, target_ref) in enumerate(
            ((owner_ref, owner), (qcl_ref, qcl), (mcl_ref, mcl), (rows_ref, rows))
        )
    ]
    for copy in small:
        copy.start()

    def load(p):
        part = pl.ds(p * piece, piece)
        return pltpu.make_async_copy(emb_ref.at[part], m_own.at[part], load_sem.at[4 + p])

    for p in range(PIECES):
        load(p).start()
    lax.fori_loop(1, 64, greet, 0)

    spread[...] = one_hot(iota((192, 192), 1) == spread_index(iota((192, 192), 0))).astype(BF16)
    gather[...] = one_hot(iota((192, 192), 0) == spread_index(iota((192, 192), 1))).astype(BF16)

    small[0].wait()
    small[1].wait()
    owners = owner[...]
    count = owners.shape[1]
    dz = ((owners >> 1) - z) & 7
    order = jnp.where(dz == 0, 0, jnp.where(dz <= 4, 2 * dz - 1, 16 - 2 * dz))
    dest = order * 8 + (((owners >> 4) - y) & 3) * 2 + ((owners - core) & 1)
    is_dest = one_hot(iota((64, count), 0) == dest)
    earlier = one_hot(iota((count, count), 0) < iota((count, count), 1)).astype(BF16)
    before = dot(is_dest.astype(BF16), earlier, (1, 0))
    rank = jnp.sum(is_dest * before, axis=0, keepdims=True).astype(jnp.int32)
    slot = dest * CAP + rank
    lane = (dest & 7) * CAP + rank
    is_lane = one_hot(iota((128, count), 0) == lane)
    labels = (jnp.concatenate([qcl[k : k + 1, :] for k in range(count // 128)], axis=1) + 1).astype(F32)
    lab_out[...] = dot((is_dest * labels).astype(BF16), is_lane.astype(BF16), (1, 1)).reshape(64, 1, 128)
    small[3].wait()
    rows[...] = unit_length(rows[...])

    def normalize(p):
        load(p).wait()

        def some(t, carry):
            part = pl.ds(pl.multiple_of(p * piece + t * 64, 64), 64)
            m_own[part, :] = unit_length(m_own[part, :])
            return carry

        lax.fori_loop(0, piece // 64, some, 0)

    def member_copy(p):
        part = pl.ds(p * piece, piece)
        return pltpu.make_async_remote_copy(
            m_own.at[part], m_par.at[part], m_s.at[p], m_r.at[p], device_id=(ex, m_mate), device_id_type=MESH
        )

    def member_label_copy():
        return pltpu.make_async_remote_copy(ml_own, ml_par, ml_s, ml_r, device_id=(ex, m_mate), device_id_type=MESH)

    def send(j):
        return pltpu.make_async_remote_copy(
            out.at[j], arrive.at[j], s_sem.at[lax.div(j, 8)], r_sem.at[lax.div(j, 8)], device_id=target(j), device_id_type=MESH
        )

    def send_label(j):
        return pltpu.make_async_remote_copy(
            lab_out.at[j], lab_in.at[j], ls_sem.at[lax.div(j, 8)], lr_sem.at[lax.div(j, 8)], device_id=target(j), device_id_type=MESH
        )

    def forward(i):
        part = pl.ds(pl.multiple_of(i * 96, 96), 96)
        return pltpu.make_async_remote_copy(
            q_own.at[part], q_par.at[part], f_s.at[i], f_r.at[i], device_id=(ex, q_mate), device_id_type=MESH
        )

    def forward_labels(h):
        return pltpu.make_async_remote_copy(
            ql_own.at[h], ql_par.at[h], fl_s.at[h], fl_r.at[h], device_id=(ex, q_mate), device_id_type=MESH
        )

    small[2].wait()
    ml_own[...] = (mcl[...] + 1).astype(F32)
    normalize(0)
    pl.semaphore_wait(barrier, 65)
    member_label_copy().start()
    member_copy(0).start()

    def place(g):
        pick = one_hot(iota((192, count), 0) + g * 192 == slot).astype(BF16)
        placed = dot(pick, rows[...], (1, 0)).astype(BF16)
        for q in range(4):
            four = placed[q * 48 : (q + 1) * 48]
            stacked = jnp.concatenate([four[:, k * 256 : (k + 1) * 256] for k in range(4)], axis=0)
            laid = dot(spread[...], stacked, (1, 0)).astype(BF16)
            for a in range(4):
                out[g * 16 + q * 4 + a] = laid[a * 48 : (a + 1) * 48]

    def start_send(j, carry):
        send(j).start()
        send_label(j).start()
        return carry

    def place_next(g, carry):
        place(g)
        lax.fori_loop(g * 16, g * 16 + 16, start_send, 0)
        return carry

    place(0)
    lax.fori_loop(1, 16, start_send, 0)
    lax.fori_loop(1, 4, place_next, 0)
    arrive[0] = out[0]
    lab_in[0] = lab_out[0]
    for p in range(1, PIECES):
        normalize(p)
        if p < 5:
            member_copy(p).start()

    def widen(row_ref, wide_ref):
        for b in range(row_ref.shape[1] // 128):
            part = jnp.broadcast_to(row_ref[:, b * 128 : (b + 1) * 128], (128, 128))
            wide_ref[b * 128 : (b + 1) * 128, :] = part.T

    widen(ml_own, mlb_own)
    c_own[...] = jnp.full(c_own.shape, -1.0, F32)
    c_par[...] = jnp.full(c_par.shape, -1.0, F32)
    r_own[...] = jnp.full(r_own.shape, -1.0, F32)
    r_par[...] = jnp.full(r_par.shape, -1.0, F32)

    def settle(ref, sem, i, first):
        part = ref.at[pl.ds(i * 8 + first, 8 - first)]
        pltpu.make_async_copy(part, part, sem.at[i]).wait()

    def take(i, first):
        settle(arrive, r_sem, i, first)
        for h in range(2):
            block = arrive[pl.ds(i * 8 + h * 4, 4)].reshape(192, 256)
            back = dot(gather[...], block, (1, 0)).astype(BF16)
            part = pl.ds(pl.multiple_of(i * 96 + h * 48, 48), 48)
            for k in range(4):
                q_own[part, k * 256 : (k + 1) * 256] = back[k * 48 : (k + 1) * 48]
        forward(i).start()

    def take_next(i, carry):
        take(i, 0)
        return carry


    def take_labels(h):
        parts = []
        for i in range(h * 4, h * 4 + 4):
            settle(lab_in, lr_sem, i, 1 if i == 0 else 0)
            parts.append(jnp.sum(lab_in[i * 8 : i * 8 + 8], axis=0)[:, :96])
        ql_own[h] = jnp.concatenate(parts, axis=1)
        forward_labels(h).start()

    def take_forward(i, carry):
        forward(i).wait_recv()
        return carry

    def score(q_ref, ql_ref, row_ref, chunks, m_ref, mlb_ref, col_ref, first, rows):
        width, start = 96 * len(chunks), 96 * chunks[0]
        step = min(rows, 512)
        label_row = jnp.concatenate([ql_ref[h] for h in range(chunks[0] // 4, chunks[-1] // 4 + 1)], axis=1)

        def tile(t, best):
            at = pl.ds(pl.multiple_of(first + t * step, 256), step)
            cosine = dot(m_ref[at, :], q_ref[start : start + width, :], (1, 1))
            wide = mlb_ref[at, :]
            parts = []
            for k in range(0, width, 128):
                n = min(128, width - k)
                value = jnp.where(wide[:, :n] == label_row[:, k : k + n], cosine[:, k : k + n], -1.0)
                col_ref[at, :n] = jnp.maximum(col_ref[at, :n], value)
                parts.append(jnp.max(value.reshape(step // 8, 8, n), axis=0))
            return jnp.maximum(best, jnp.concatenate(parts, axis=1))

        best = lax.fori_loop(0, rows // step, tile, jnp.full((8, width), -1.0, F32))
        best = jnp.max(best, axis=0, keepdims=True)
        for k, i in enumerate(chunks):
            row_ref[i, :, :96] = jnp.maximum(row_ref[i, :, :96], best[:, k * 96 : (k + 1) * 96])

    members = m_own.shape[0]
    whole, low, high = range(8), range(4), range(4, 8)

    def score_own(q_ref, ql_ref, row_ref, chunks):
        score(q_ref, ql_ref, row_ref, chunks, m_own, mlb_own, c_own, 0, members)

    def score_pieces(q_ref, ql_ref, row_ref, chunks, first, last):
        score(q_ref, ql_ref, row_ref, chunks, m_par, mlb_par, c_par, first * piece, (last - first) * piece)

    def members_in(first, last):
        for p in range(first, last):
            member_copy(p).wait_recv()

    take(0, 1)
    lax.fori_loop(1, 4, take_next, 0)
    take_labels(0)
    score_own(q_own, ql_own, r_own, low)
    take(4, 0)
    member_label_copy().wait_recv()
    widen(ml_par, mlb_par)
    forward_labels(0).wait_recv()
    take(5, 0)
    lax.fori_loop(0, 4, take_forward, 0)
    score_own(q_par, ql_par, r_par, low)
    take(6, 0)
    members_in(0, 2)
    score_pieces(q_own, ql_own, r_own, low, 0, 2)
    score_pieces(q_par, ql_par, r_par, low, 0, 2)
    take(7, 0)
    take_labels(1)
    score_own(q_own, ql_own, r_own, high)
    forward(6).wait_send()
    member_copy(5).start()
    score_pieces(q_own, ql_own, r_own, high, 0, 2)
    members_in(2, 4)
    score_pieces(q_own, ql_own, r_own, whole, 2, 4)
    score_pieces(q_par, ql_par, r_par, low, 2, 4)
    forward_labels(1).wait_recv()
    lax.fori_loop(4, 8, take_forward, 0)
    score_own(q_par, ql_par, r_par, high)
    score_pieces(q_par, ql_par, r_par, high, 0, 4)
    for p in range(4, PIECES):
        members_in(p, p + 1)
        score_pieces(q_par, ql_par, r_par, whole, p, p + 1)
        if p == PIECES - 1:
            trade = pltpu.make_async_remote_copy(r_par, r_got, b_s, b_r, device_id=(ex, q_mate), device_id_type=MESH)
            trade.start()
        score_pieces(q_own, ql_own, r_own, whole, p, p + 1)

    def columns_of(col_ref, b):
        return jnp.max(col_ref[b * 128 : (b + 1) * 128, :].T, axis=0, keepdims=True)

    def answer_z(i):
        return pltpu.make_async_remote_copy(
            ret_out.at[i], ret_mid.at[i], tz_s.at[i], tz_r, device_id=place_at(0, 8 - shift(8 * i)[1], 0), device_id_type=MESH
        )

    def answer_y(k):
        return pltpu.make_async_remote_copy(
            ret_mid, ret_in.at[k], t_s.at[k], t_r, device_id=place_at(4 - k // 2, 0, 2 - k % 2), device_id_type=MESH
        )

    trade.wait_recv()
    for i in range(1, 8):
        ret_out[i] = jnp.maximum(r_own[i], r_got[i])
        answer_z(i).start()
    ret_mid[0] = jnp.maximum(r_own[0], r_got[0])
    blocks = members // 128
    for b in range(blocks):
        c_send[:, b * 128 : (b + 1) * 128] = columns_of(c_par, b)
    columns = pltpu.make_async_remote_copy(c_send, c_got, c_s, c_r, device_id=(ex, m_mate), device_id_type=MESH)
    columns.start()
    far = ret_mid.at[pl.ds(1, 7)]
    pltpu.make_async_copy(far, far, tz_r).wait()
    for k in range(1, 8):
        answer_y(k).start()
    ret_in[0] = ret_mid[...]
    for b in range(blocks):
        rmax_ref[:, b * 128 : (b + 1) * 128] = columns_of(c_own, b)

    for i in range(8):
        first = 1 if i == 0 else 0
        settle(out, s_sem, i, first)
        settle(lab_out, ls_sem, i, first)
        if i != 6:
            forward(i).wait_send()
    for h in range(2):
        forward_labels(h).wait_send()
    member_label_copy().wait_send()
    for p in range(PIECES):
        member_copy(p).wait_send()
    trade.wait_send()

    for k in range(1, 8):
        answer_z(k).wait_send()
        answer_y(k).wait_send()
    answers = ret_in.at[pl.ds(1, 7)]
    pltpu.make_async_copy(answers, answers, t_r).wait()
    by_row = one_hot(iota((64, count), 0) == (dest & 7) * 8 + (dest >> 3))
    by_lane = dot(ret_in[...].reshape(64, 128), by_row, (0, 0), EXACT)
    qmax_ref[...] = jnp.sum(by_lane * is_lane, axis=0, keepdims=True)
    columns.wait()
    rmax_ref[...] = jnp.maximum(rmax_ref[...], c_got[...])


def shards(embeddings, block_rows, owners, query_cluster, member_cluster):
    members, width = embeddings.shape
    count = block_rows.shape[0]
    vmem = pl.BlockSpec(memory_space=pltpu.VMEM)
    dma = pltpu.SemaphoreType.DMA
    v = pltpu.VMEM
    query_max, resident_max = pl.pallas_call(
        kernel,
        out_shape=(pltpu.VMEM((1, count), F32), pltpu.VMEM((1, members), F32)),
        in_specs=[pl.BlockSpec(memory_space=pl.ANY)] * 5,
        out_specs=(vmem, vmem),
        scratch_shapes=[
            v((count, width), BF16), v((1, count), jnp.int32), v((count // 128, 128), jnp.int32), v((1, members), jnp.int32),
            v((192, 192), BF16), v((192, 192), BF16),
            v((64, 48, 256), BF16), v((64, 48, 256), BF16), v((64, 1, 128), F32), v((64, 1, 128), F32),
            v((768, width), BF16), v((768, width), BF16), v((2, 1, 384), F32), v((2, 1, 384), F32),
            v((members, width), BF16), v((members, width), BF16), v((1, members), F32), v((1, members), F32),
            v((members, 128), F32), v((members, 128), F32),
            v((8, 1, 128), F32), v((8, 1, 128), F32), v((8, 1, 128), F32),
            v((members, 128), F32), v((members, 128), F32), v((1, members), F32), v((1, members), F32),
            v((8, 1, 128), F32), v((8, 1, 128), F32), v((8, 8, 1, 128), F32),
            dma((4 + PIECES,)),
            dma((8,)), dma((8,)), dma((8,)), dma((8,)),
            dma((8,)), dma((8,)), dma((2,)), dma((2,)),
            dma((PIECES,)), dma((PIECES,)), dma, dma,
            dma, dma, dma, dma, dma((8,)), dma, dma((8,)), dma,
        ],
        compiler_params=pltpu.CompilerParams(collective_id=0, has_side_effects=True, vmem_limit_bytes=56 << 20),
    )(
        embeddings,
        block_rows,
        owners.reshape(1, count),
        query_cluster.reshape(count // 128, 128),
        member_cluster,
    )
    return query_max.reshape(count), resident_max.reshape(members)


def solution(mesh):
    placed = (
        P(("ex", "rep"), None),
        P(("ex", "rep"), None),
        P(("ex", "rep"), None),
        P(("ex", "rep")),
        P("ex", "rep"),
    )
    return jax.shard_map(
        shards,
        mesh=mesh,
        in_specs=placed,
        out_specs=(P(("ex", "rep")), P(("ex", "rep"))),
        check_vma=False,
    )
```

```python
import jax
import jax.numpy as jnp
from jax import lax
from jax.experimental import pallas as pl
from jax.experimental.pallas import tpu as pltpu
from jax.sharding import PartitionSpec as P

MESH = pl.DeviceIdType.MESH
F32, BF16 = jnp.float32, jnp.bfloat16
EXACT = lax.Precision.HIGHEST
CAP = 12
PIECES = 6


def unit_length(block):
    wide = block.astype(F32)
    squares = jnp.sum(wide * wide, axis=1, keepdims=True)
    return (wide * lax.rsqrt(squares + 1e-06)).astype(BF16)


def dot(a, b, contract, precision=None):
    return lax.dot_general(a, b, ((contract[:1], contract[1:]), ((), ())), preferred_element_type=F32, precision=precision)


def iota(shape, axis):
    return lax.broadcasted_iota(jnp.int32, shape, axis)


def one_hot(match):
    return jnp.where(match, 1.0, 0.0)


def spread_index(r):
    a = (r * 1366) >> 16
    rest = r - a * 48
    k = (rest * 5462) >> 16
    return k * 48 + a * CAP + rest - k * CAP


def kernel(
    emb_ref, rows_ref, owner_ref, qcl_ref, mcl_ref,
    qmax_ref, rmax_ref,
    rows, owner, qcl, mcl, spread, gather,
    out, arrive, lab_out, lab_in, q_own, q_par, ql_own, ql_par, m_own, m_par, ml_own, ml_par, mlb_own, mlb_par,
    r_own, r_par, mid_own, mid_par, c_own, c_par, c_send, c_got, ret_mid, ret_in,
    load_sem, s_sem, r_sem, ls_sem, lr_sem, f_s, f_r, fl_s, fl_r, m_s, m_r, ml_s, ml_r, b_s, b_r, c_s, c_r, tz_s, tz_r, t_s, t_r,
):
    ex, rep = lax.axis_index("ex"), lax.axis_index("rep")
    core, z, y = lax.rem(ex, 2), lax.rem(lax.div(ex, 2), 8), lax.div(ex, 16)
    near = rep + 1 - 2 * lax.rem(rep, 2)
    m_mate = (1 - core) * near + core * (3 - rep)
    q_mate = (1 - core) * (3 - rep) + core * near

    def place_at(dy, dz, dc):
        return ((lax.rem(y + dy, 4) * 8 + lax.rem(z + dz, 8)) * 2 + lax.rem(core + dc, 2), rep)

    def shift(j):
        if isinstance(j, int):
            i = j // 8
            return (j // 2) % 4, ((i + 1) // 2 if i % 2 else (8 - i // 2) % 8), j % 2
        i = lax.div(j, 8)
        odd = lax.rem(i, 2)
        half = lax.div(i + 1, 2)
        return lax.rem(lax.div(j, 2), 4), odd * half + (1 - odd) * lax.rem(8 - half, 8), lax.rem(j, 2)

    def target(j):
        return place_at(*shift(j))

    barrier = pltpu.get_barrier_semaphore()

    def greet(j, carry):
        pl.semaphore_signal(barrier, inc=1, device_id=target(j), device_id_type=MESH)
        return carry

    for mate in (m_mate, q_mate):
        pl.semaphore_signal(barrier, inc=1, device_id=(ex, mate), device_id_type=MESH)
    for k in range(1, 8):
        pl.semaphore_signal(barrier, inc=1, device_id=(place_at(0, k, 0)[0], q_mate), device_id_type=MESH)

    piece = m_own.shape[0] // PIECES
    small = [
        pltpu.make_async_copy(source, target_ref, load_sem.at[k])
        for k, (source, target_ref) in enumerate(
            ((owner_ref, owner), (qcl_ref, qcl), (mcl_ref, mcl), (rows_ref, rows))
        )
    ]
    for copy in small:
        copy.start()

    def load(p):
        part = pl.ds(p * piece, piece)
        return pltpu.make_async_copy(emb_ref.at[part], m_own.at[part], load_sem.at[4 + p])

    for p in range(PIECES):
        load(p).start()
    lax.fori_loop(1, 64, greet, 0)

    spread[...] = one_hot(iota((192, 192), 1) == spread_index(iota((192, 192), 0))).astype(BF16)
    gather[...] = one_hot(iota((192, 192), 0) == spread_index(iota((192, 192), 1))).astype(BF16)

    small[0].wait()
    small[1].wait()
    owners = owner[...]
    count = owners.shape[1]
    dz = ((owners >> 1) - z) & 7
    order = jnp.where(dz == 0, 0, jnp.where(dz <= 4, 2 * dz - 1, 16 - 2 * dz))
    dest = order * 8 + (((owners >> 4) - y) & 3) * 2 + ((owners - core) & 1)
    is_dest = one_hot(iota((64, count), 0) == dest)
    earlier = one_hot(iota((count, count), 0) < iota((count, count), 1)).astype(BF16)
    before = dot(is_dest.astype(BF16), earlier, (1, 0))
    rank = jnp.sum(is_dest * before, axis=0, keepdims=True).astype(jnp.int32)
    slot = dest * CAP + rank
    lane = (dest & 7) * CAP + rank
    is_lane = one_hot(iota((128, count), 0) == lane)
    labels = (jnp.concatenate([qcl[k : k + 1, :] for k in range(count // 128)], axis=1) + 1).astype(F32)
    lab_out[...] = dot((is_dest * labels).astype(BF16), is_lane.astype(BF16), (1, 1)).reshape(64, 1, 128)
    small[3].wait()
    rows[...] = unit_length(rows[...])

    def normalize(p):
        load(p).wait()

        def some(t, carry):
            part = pl.ds(pl.multiple_of(p * piece + t * 64, 64), 64)
            m_own[part, :] = unit_length(m_own[part, :])
            return carry

        lax.fori_loop(0, piece // 64, some, 0)

    def member_copy(p):
        part = pl.ds(p * piece, piece)
        return pltpu.make_async_remote_copy(
            m_own.at[part], m_par.at[part], m_s.at[p], m_r.at[p], device_id=(ex, m_mate), device_id_type=MESH
        )

    def member_label_copy():
        return pltpu.make_async_remote_copy(ml_own, ml_par, ml_s, ml_r, device_id=(ex, m_mate), device_id_type=MESH)

    def send(j):
        return pltpu.make_async_remote_copy(
            out.at[j], arrive.at[j], s_sem.at[lax.div(j, 8)], r_sem.at[lax.div(j, 8)], device_id=target(j), device_id_type=MESH
        )

    def send_label(j):
        return pltpu.make_async_remote_copy(
            lab_out.at[j], lab_in.at[j], ls_sem.at[lax.div(j, 8)], lr_sem.at[lax.div(j, 8)], device_id=target(j), device_id_type=MESH
        )

    def forward(i):
        part = pl.ds(pl.multiple_of(i * 96, 96), 96)
        return pltpu.make_async_remote_copy(
            q_own.at[part], q_par.at[part], f_s.at[i], f_r.at[i], device_id=(ex, q_mate), device_id_type=MESH
        )

    def forward_labels(h):
        return pltpu.make_async_remote_copy(
            ql_own.at[h], ql_par.at[h], fl_s.at[h], fl_r.at[h], device_id=(ex, q_mate), device_id_type=MESH
        )

    small[2].wait()
    ml_own[...] = (mcl[...] + 1).astype(F32)
    normalize(0)
    pl.semaphore_wait(barrier, 72)
    member_label_copy().start()
    member_copy(0).start()

    def place(g):
        pick = one_hot(iota((192, count), 0) + g * 192 == slot).astype(BF16)
        placed = dot(pick, rows[...], (1, 0)).astype(BF16)
        for q in range(4):
            four = placed[q * 48 : (q + 1) * 48]
            stacked = jnp.concatenate([four[:, k * 256 : (k + 1) * 256] for k in range(4)], axis=0)
            laid = dot(spread[...], stacked, (1, 0)).astype(BF16)
            for a in range(4):
                out[g * 16 + q * 4 + a] = laid[a * 48 : (a + 1) * 48]

    def start_send(j, carry):
        send(j).start()
        send_label(j).start()
        return carry

    def place_next(g, carry):
        place(g)
        lax.fori_loop(g * 16, g * 16 + 16, start_send, 0)
        return carry

    place(0)
    lax.fori_loop(1, 16, start_send, 0)
    lax.fori_loop(1, 4, place_next, 0)
    arrive[0] = out[0]
    lab_in[0] = lab_out[0]
    for p in range(1, PIECES):
        normalize(p)
        if p < 5:
            member_copy(p).start()

    def widen(row_ref, wide_ref):
        for b in range(row_ref.shape[1] // 128):
            part = jnp.broadcast_to(row_ref[:, b * 128 : (b + 1) * 128], (128, 128))
            wide_ref[b * 128 : (b + 1) * 128, :] = part.T

    widen(ml_own, mlb_own)
    c_own[...] = jnp.full(c_own.shape, -1.0, F32)
    c_par[...] = jnp.full(c_par.shape, -1.0, F32)
    r_own[...] = jnp.full(r_own.shape, -1.0, F32)
    r_par[...] = jnp.full(r_par.shape, -1.0, F32)

    def settle(ref, sem, i, first):
        part = ref.at[pl.ds(i * 8 + first, 8 - first)]
        pltpu.make_async_copy(part, part, sem.at[i]).wait()

    def take(i, first):
        settle(arrive, r_sem, i, first)
        for h in range(2):
            block = arrive[pl.ds(i * 8 + h * 4, 4)].reshape(192, 256)
            back = dot(gather[...], block, (1, 0)).astype(BF16)
            part = pl.ds(pl.multiple_of(i * 96 + h * 48, 48), 48)
            for k in range(4):
                q_own[part, k * 256 : (k + 1) * 256] = back[k * 48 : (k + 1) * 48]
        forward(i).start()

    def take_next(i, carry):
        take(i, 0)
        return carry


    def take_labels(h):
        parts = []
        for i in range(h * 4, h * 4 + 4):
            settle(lab_in, lr_sem, i, 1 if i == 0 else 0)
            parts.append(jnp.sum(lab_in[i * 8 : i * 8 + 8], axis=0)[:, :96])
        ql_own[h] = jnp.concatenate(parts, axis=1)
        forward_labels(h).start()

    def take_forward(i, carry):
        forward(i).wait_recv()
        return carry

    def score(q_ref, ql_ref, row_ref, chunks, m_ref, mlb_ref, col_ref, first, rows):
        width, start = 96 * len(chunks), 96 * chunks[0]
        step = min(rows, 512)
        label_row = jnp.concatenate([ql_ref[h] for h in range(chunks[0] // 4, chunks[-1] // 4 + 1)], axis=1)

        def tile(t, best):
            at = pl.ds(pl.multiple_of(first + t * step, 256), step)
            cosine = dot(m_ref[at, :], q_ref[start : start + width, :], (1, 1))
            wide = mlb_ref[at, :]
            parts = []
            for k in range(0, width, 128):
                n = min(128, width - k)
                value = jnp.where(wide[:, :n] == label_row[:, k : k + n], cosine[:, k : k + n], -1.0)
                col_ref[at, :n] = jnp.maximum(col_ref[at, :n], value)
                parts.append(jnp.max(value.reshape(step // 8, 8, n), axis=0))
            return jnp.maximum(best, jnp.concatenate(parts, axis=1))

        best = lax.fori_loop(0, rows // step, tile, jnp.full((8, width), -1.0, F32))
        best = jnp.max(best, axis=0, keepdims=True)
        for k, i in enumerate(chunks):
            row_ref[i, :, :96] = jnp.maximum(row_ref[i, :, :96], best[:, k * 96 : (k + 1) * 96])

    members = m_own.shape[0]
    whole, low, high = range(8), range(4), range(4, 8)

    def score_own(q_ref, ql_ref, row_ref, chunks):
        score(q_ref, ql_ref, row_ref, chunks, m_own, mlb_own, c_own, 0, members)

    def score_pieces(q_ref, ql_ref, row_ref, chunks, first, last):
        score(q_ref, ql_ref, row_ref, chunks, m_par, mlb_par, c_par, first * piece, (last - first) * piece)

    def members_in(first, last):
        for p in range(first, last):
            member_copy(p).wait_recv()

    take(0, 1)
    lax.fori_loop(1, 4, take_next, 0)
    take_labels(0)
    score_own(q_own, ql_own, r_own, low)
    take(4, 0)
    member_label_copy().wait_recv()
    widen(ml_par, mlb_par)
    forward_labels(0).wait_recv()
    take(5, 0)
    lax.fori_loop(0, 4, take_forward, 0)
    score_own(q_par, ql_par, r_par, low)
    take(6, 0)
    members_in(0, 2)
    score_pieces(q_own, ql_own, r_own, low, 0, 2)
    score_pieces(q_par, ql_par, r_par, low, 0, 2)
    take(7, 0)
    take_labels(1)
    score_own(q_own, ql_own, r_own, high)
    forward(6).wait_send()
    member_copy(5).start()
    score_pieces(q_own, ql_own, r_own, high, 0, 2)
    members_in(2, 4)
    score_pieces(q_own, ql_own, r_own, whole, 2, 4)
    score_pieces(q_par, ql_par, r_par, low, 2, 4)
    forward_labels(1).wait_recv()
    lax.fori_loop(4, 8, take_forward, 0)
    score_own(q_par, ql_par, r_par, high)
    score_pieces(q_par, ql_par, r_par, high, 0, 4)
    def answer_z(i):
        return pltpu.make_async_remote_copy(
            r_own.at[i], mid_own.at[i], tz_s.at[i], tz_r, device_id=place_at(0, 8 - shift(8 * i)[1], 0), device_id_type=MESH
        )

    def answer_x(i):
        there = place_at(0, 8 - shift(8 * i)[1], 0)[0] if i else ex
        return pltpu.make_async_remote_copy(
            r_par.at[i], mid_par.at[i], b_s.at[i], b_r, device_id=(there, q_mate), device_id_type=MESH
        )

    def answer_y(k):
        return pltpu.make_async_remote_copy(
            ret_mid, ret_in.at[k], t_s.at[k], t_r, device_id=place_at(4 - k // 2, 0, 2 - k % 2), device_id_type=MESH
        )

    for p in range(4, PIECES):
        members_in(p, p + 1)
        score_pieces(q_par, ql_par, r_par, whole, p, p + 1)
        if p == PIECES - 1:
            for i in range(8):
                answer_x(i).start()
        score_pieces(q_own, ql_own, r_own, whole, p, p + 1)

    def columns_of(col_ref, b):
        return jnp.max(col_ref[b * 128 : (b + 1) * 128, :].T, axis=0, keepdims=True)

    for i in range(1, 8):
        answer_z(i).start()
    mid_own[0] = r_own[0]
    blocks = members // 128
    for b in range(blocks):
        c_send[:, b * 128 : (b + 1) * 128] = columns_of(c_par, b)
    columns = pltpu.make_async_remote_copy(c_send, c_got, c_s, c_r, device_id=(ex, m_mate), device_id_type=MESH)
    columns.start()
    far = mid_own.at[pl.ds(1, 7)]
    pltpu.make_async_copy(far, far, tz_r).wait()
    pltpu.make_async_copy(mid_par, mid_par, b_r).wait()
    ret_mid[...] = jnp.maximum(mid_own[...], mid_par[...])
    for k in range(1, 8):
        answer_y(k).start()
    ret_in[0] = ret_mid[...]
    for b in range(blocks):
        rmax_ref[:, b * 128 : (b + 1) * 128] = columns_of(c_own, b)

    for i in range(8):
        first = 1 if i == 0 else 0
        settle(out, s_sem, i, first)
        settle(lab_out, ls_sem, i, first)
        if i != 6:
            forward(i).wait_send()
    for h in range(2):
        forward_labels(h).wait_send()
    member_label_copy().wait_send()
    for p in range(PIECES):
        member_copy(p).wait_send()
    for i in range(8):
        answer_x(i).wait_send()

    for k in range(1, 8):
        answer_z(k).wait_send()
        answer_y(k).wait_send()
    answers = ret_in.at[pl.ds(1, 7)]
    pltpu.make_async_copy(answers, answers, t_r).wait()
    by_row = one_hot(iota((64, count), 0) == (dest & 7) * 8 + (dest >> 3))
    by_lane = dot(ret_in[...].reshape(64, 128), by_row, (0, 0), EXACT)
    qmax_ref[...] = jnp.sum(by_lane * is_lane, axis=0, keepdims=True)
    columns.wait()
    rmax_ref[...] = jnp.maximum(rmax_ref[...], c_got[...])


def shards(embeddings, block_rows, owners, query_cluster, member_cluster):
    members, width = embeddings.shape
    count = block_rows.shape[0]
    vmem = pl.BlockSpec(memory_space=pltpu.VMEM)
    dma = pltpu.SemaphoreType.DMA
    v = pltpu.VMEM
    query_max, resident_max = pl.pallas_call(
        kernel,
        out_shape=(pltpu.VMEM((1, count), F32), pltpu.VMEM((1, members), F32)),
        in_specs=[pl.BlockSpec(memory_space=pl.ANY)] * 5,
        out_specs=(vmem, vmem),
        scratch_shapes=[
            v((count, width), BF16), v((1, count), jnp.int32), v((count // 128, 128), jnp.int32), v((1, members), jnp.int32),
            v((192, 192), BF16), v((192, 192), BF16),
            v((64, 48, 256), BF16), v((64, 48, 256), BF16), v((64, 1, 128), F32), v((64, 1, 128), F32),
            v((768, width), BF16), v((768, width), BF16), v((2, 1, 384), F32), v((2, 1, 384), F32),
            v((members, width), BF16), v((members, width), BF16), v((1, members), F32), v((1, members), F32),
            v((members, 128), F32), v((members, 128), F32),
            v((8, 1, 128), F32), v((8, 1, 128), F32), v((8, 1, 128), F32), v((8, 1, 128), F32),
            v((members, 128), F32), v((members, 128), F32), v((1, members), F32), v((1, members), F32),
            v((8, 1, 128), F32), v((8, 8, 1, 128), F32),
            dma((4 + PIECES,)),
            dma((8,)), dma((8,)), dma((8,)), dma((8,)),
            dma((8,)), dma((8,)), dma((2,)), dma((2,)),
            dma((PIECES,)), dma((PIECES,)), dma, dma,
            dma((8,)), dma, dma, dma, dma((8,)), dma, dma((8,)), dma,
        ],
        compiler_params=pltpu.CompilerParams(collective_id=0, has_side_effects=True, vmem_limit_bytes=56 << 20),
    )(
        embeddings,
        block_rows,
        owners.reshape(1, count),
        query_cluster.reshape(count // 128, 128),
        member_cluster,
    )
    return query_max.reshape(count), resident_max.reshape(members)


def solution(mesh):
    placed = (
        P(("ex", "rep"), None),
        P(("ex", "rep"), None),
        P(("ex", "rep"), None),
        P(("ex", "rep")),
        P("ex", "rep"),
    )
    return jax.shard_map(
        shards,
        mesh=mesh,
        in_specs=placed,
        out_specs=(P(("ex", "rep")), P(("ex", "rep"))),
        check_vma=False,
    )
```

```python
import jax
import jax.numpy as jnp
from jax import lax
from jax.experimental import pallas as pl
from jax.experimental.pallas import tpu as pltpu
from jax.sharding import PartitionSpec as P

MESH = pl.DeviceIdType.MESH
F32, BF16 = jnp.float32, jnp.bfloat16
EXACT = lax.Precision.HIGHEST
CAP = 12
PIECES = 6


def unit_length(block):
    wide = block.astype(F32)
    squares = jnp.sum(wide * wide, axis=1, keepdims=True)
    return (wide * lax.rsqrt(squares + 1e-06)).astype(BF16)


def dot(a, b, contract, precision=None):
    return lax.dot_general(a, b, ((contract[:1], contract[1:]), ((), ())), preferred_element_type=F32, precision=precision)


def iota(shape, axis):
    return lax.broadcasted_iota(jnp.int32, shape, axis)


def one_hot(match):
    return jnp.where(match, 1.0, 0.0)


def spread_index(r):
    a = (r * 1366) >> 16
    rest = r - a * 48
    k = (rest * 5462) >> 16
    return k * 48 + a * CAP + rest - k * CAP


def kernel(
    emb_ref, rows_ref, owner_ref, qcl_ref, mcl_ref,
    qmax_ref, rmax_ref,
    rows, owner, qcl, mcl, spread, gather,
    out, arrive, lab_out, lab_in, q_own, q_par, ql_own, ql_par, m_own, m_par, ml_own, ml_par, mlb_own, mlb_par,
    r_own, r_par, mid_own, mid_par, c_own, c_par, c_send, c_got, ret_mid, ret_in,
    load_sem, s_sem, r_sem, ls_sem, lr_sem, f_s, f_r, fl_s, fl_r, m_s, m_r, ml_s, ml_r, b_s, b_r, c_s, c_r, tz_s, tz_r, t_s, t_r,
):
    ex, rep = lax.axis_index("ex"), lax.axis_index("rep")
    core, z, y = lax.rem(ex, 2), lax.rem(lax.div(ex, 2), 8), lax.div(ex, 16)
    near = rep + 1 - 2 * lax.rem(rep, 2)
    m_mate = (1 - core) * near + core * (3 - rep)
    q_mate = (1 - core) * (3 - rep) + core * near

    def place_at(dy, dz, dc):
        return ((lax.rem(y + dy, 4) * 8 + lax.rem(z + dz, 8)) * 2 + lax.rem(core + dc, 2), rep)

    def shift(j):
        if isinstance(j, int):
            i = j // 8
            return (j // 2) % 4, ((i + 1) // 2 if i % 2 else (8 - i // 2) % 8), j % 2
        i = lax.div(j, 8)
        odd = lax.rem(i, 2)
        half = lax.div(i + 1, 2)
        return lax.rem(lax.div(j, 2), 4), odd * half + (1 - odd) * lax.rem(8 - half, 8), lax.rem(j, 2)

    def target(j):
        return place_at(*shift(j))

    barrier = pltpu.get_barrier_semaphore()

    def greet(j, carry):
        pl.semaphore_signal(barrier, inc=1, device_id=target(j), device_id_type=MESH)
        return carry

    for mate in (m_mate, q_mate):
        pl.semaphore_signal(barrier, inc=1, device_id=(ex, mate), device_id_type=MESH)
    for k in range(1, 8):
        pl.semaphore_signal(barrier, inc=1, device_id=(place_at(0, k, 0)[0], q_mate), device_id_type=MESH)

    piece = m_own.shape[0] // PIECES
    small = [
        pltpu.make_async_copy(source, target_ref, load_sem.at[k])
        for k, (source, target_ref) in enumerate(
            ((owner_ref, owner), (qcl_ref, qcl), (mcl_ref, mcl), (rows_ref, rows))
        )
    ]
    for copy in small:
        copy.start()

    def load(p):
        part = pl.ds(p * piece, piece)
        return pltpu.make_async_copy(emb_ref.at[part], m_own.at[part], load_sem.at[4 + p])

    for p in range(PIECES):
        load(p).start()
    lax.fori_loop(1, 64, greet, 0)

    spread[...] = one_hot(iota((192, 192), 1) == spread_index(iota((192, 192), 0))).astype(BF16)
    gather[...] = one_hot(iota((192, 192), 0) == spread_index(iota((192, 192), 1))).astype(BF16)

    small[0].wait()
    small[1].wait()
    owners = owner[...]
    count = owners.shape[1]
    dz = ((owners >> 1) - z) & 7
    order = jnp.where(dz == 0, 0, jnp.where(dz <= 4, 2 * dz - 1, 16 - 2 * dz))
    dest = order * 8 + (((owners >> 4) - y) & 3) * 2 + ((owners - core) & 1)
    is_dest = one_hot(iota((64, count), 0) == dest)
    earlier = one_hot(iota((count, count), 0) < iota((count, count), 1)).astype(BF16)
    before = dot(is_dest.astype(BF16), earlier, (1, 0))
    rank = jnp.sum(is_dest * before, axis=0, keepdims=True).astype(jnp.int32)
    slot = dest * CAP + rank
    lane = (dest & 7) * CAP + rank
    is_lane = one_hot(iota((128, count), 0) == lane)
    labels = (jnp.concatenate([qcl[k : k + 1, :] for k in range(count // 128)], axis=1) + 1).astype(F32)
    lab_out[...] = dot((is_dest * labels).astype(BF16), is_lane.astype(BF16), (1, 1)).reshape(64, 1, 128)
    small[3].wait()
    rows[...] = unit_length(rows[...])

    def normalize(p):
        load(p).wait()

        def some(t, carry):
            part = pl.ds(pl.multiple_of(p * piece + t * 64, 64), 64)
            m_own[part, :] = unit_length(m_own[part, :])
            return carry

        lax.fori_loop(0, piece // 64, some, 0)

    def member_copy(p):
        part = pl.ds(p * piece, piece)
        return pltpu.make_async_remote_copy(
            m_own.at[part], m_par.at[part], m_s.at[p], m_r.at[p], device_id=(ex, m_mate), device_id_type=MESH
        )

    def member_label_copy():
        return pltpu.make_async_remote_copy(ml_own, ml_par, ml_s, ml_r, device_id=(ex, m_mate), device_id_type=MESH)

    def send(j):
        return pltpu.make_async_remote_copy(
            out.at[j], arrive.at[j], s_sem.at[lax.div(j, 8)], r_sem.at[lax.div(j, 8)], device_id=target(j), device_id_type=MESH
        )

    def send_label(j):
        return pltpu.make_async_remote_copy(
            lab_out.at[j], lab_in.at[j], ls_sem.at[lax.div(j, 8)], lr_sem.at[lax.div(j, 8)], device_id=target(j), device_id_type=MESH
        )

    def forward(i):
        part = pl.ds(pl.multiple_of(i * 96, 96), 96)
        return pltpu.make_async_remote_copy(
            q_own.at[part], q_par.at[part], f_s.at[i], f_r.at[i], device_id=(ex, q_mate), device_id_type=MESH
        )

    def forward_labels(h):
        return pltpu.make_async_remote_copy(
            ql_own.at[h], ql_par.at[h], fl_s.at[h], fl_r.at[h], device_id=(ex, q_mate), device_id_type=MESH
        )

    small[2].wait()
    ml_own[...] = (mcl[...] + 1).astype(F32)
    normalize(0)
    pl.semaphore_wait(barrier, 72)
    member_label_copy().start()
    member_copy(0).start()

    def place(g):
        pick = one_hot(iota((192, count), 0) + g * 192 == slot).astype(BF16)
        placed = dot(pick, rows[...], (1, 0)).astype(BF16)
        for q in range(4):
            four = placed[q * 48 : (q + 1) * 48]
            stacked = jnp.concatenate([four[:, k * 256 : (k + 1) * 256] for k in range(4)], axis=0)
            laid = dot(spread[...], stacked, (1, 0)).astype(BF16)
            for a in range(4):
                out[g * 16 + q * 4 + a] = laid[a * 48 : (a + 1) * 48]

    def start_send(j, carry):
        send(j).start()
        send_label(j).start()
        return carry

    def place_next(g, carry):
        place(g)
        lax.fori_loop(g * 16, g * 16 + 16, start_send, 0)
        return carry

    place(0)
    lax.fori_loop(1, 16, start_send, 0)
    lax.fori_loop(1, 4, place_next, 0)
    arrive[0] = out[0]
    lab_in[0] = lab_out[0]
    for p in range(1, PIECES):
        normalize(p)
        if p < 5:
            member_copy(p).start()

    def widen(row_ref, wide_ref):
        for b in range(row_ref.shape[1] // 128):
            part = jnp.broadcast_to(row_ref[:, b * 128 : (b + 1) * 128], (128, 128))
            wide_ref[b * 128 : (b + 1) * 128, :] = part.T

    widen(ml_own, mlb_own)
    c_own[...] = jnp.full(c_own.shape, -1.0, F32)
    c_par[...] = jnp.full(c_par.shape, -1.0, F32)
    r_own[...] = jnp.full(r_own.shape, -1.0, F32)
    r_par[...] = jnp.full(r_par.shape, -1.0, F32)

    def settle(ref, sem, i, first):
        part = ref.at[pl.ds(i * 8 + first, 8 - first)]
        pltpu.make_async_copy(part, part, sem.at[i]).wait()

    def take(i, first):
        settle(arrive, r_sem, i, first)
        for h in range(2):
            block = arrive[pl.ds(i * 8 + h * 4, 4)].reshape(192, 256)
            back = dot(gather[...], block, (1, 0)).astype(BF16)
            part = pl.ds(pl.multiple_of(i * 96 + h * 48, 48), 48)
            for k in range(4):
                q_own[part, k * 256 : (k + 1) * 256] = back[k * 48 : (k + 1) * 48]
        forward(i).start()

    def take_next(i, carry):
        take(i, 0)
        return carry


    def take_labels(h):
        parts = []
        for i in range(h * 4, h * 4 + 4):
            settle(lab_in, lr_sem, i, 1 if i == 0 else 0)
            parts.append(jnp.sum(lab_in[i * 8 : i * 8 + 8], axis=0)[:, :96])
        ql_own[h] = jnp.concatenate(parts, axis=1)
        forward_labels(h).start()

    def take_forward(i, carry):
        forward(i).wait_recv()
        return carry

    def score(q_ref, ql_ref, row_ref, chunks, m_ref, mlb_ref, col_ref, first, rows):
        width, start = 96 * len(chunks), 96 * chunks[0]
        step = rows if width < 500 and rows <= 1024 else min(rows, 768 if rows == 1536 else 512)
        label_row = jnp.concatenate([ql_ref[h] for h in range(chunks[0] // 4, chunks[-1] // 4 + 1)], axis=1)

        def tile(t, best):
            at = pl.ds(pl.multiple_of(first + t * step, 256), step)
            cosine = dot(m_ref[at, :], q_ref[start : start + width, :], (1, 1))
            wide = mlb_ref[at, :]
            parts = []
            for k in range(0, width, 128):
                n = min(128, width - k)
                value = jnp.where(wide[:, :n] == label_row[:, k : k + n], cosine[:, k : k + n], -1.0)
                col_ref[at, :n] = jnp.maximum(col_ref[at, :n], value)
                parts.append(jnp.max(value.reshape(step // 8, 8, n), axis=0))
            return jnp.maximum(best, jnp.concatenate(parts, axis=1))

        best = lax.fori_loop(0, rows // step, tile, jnp.full((8, width), -1.0, F32))
        best = jnp.max(best, axis=0, keepdims=True)
        for k, i in enumerate(chunks):
            row_ref[i, :, :96] = jnp.maximum(row_ref[i, :, :96], best[:, k * 96 : (k + 1) * 96])

    members = m_own.shape[0]
    whole, low, high = range(8), range(4), range(4, 8)

    def score_own(q_ref, ql_ref, row_ref, chunks):
        score(q_ref, ql_ref, row_ref, chunks, m_own, mlb_own, c_own, 0, members)

    def score_pieces(q_ref, ql_ref, row_ref, chunks, first, last):
        score(q_ref, ql_ref, row_ref, chunks, m_par, mlb_par, c_par, first * piece, (last - first) * piece)

    def members_in(first, last):
        for p in range(first, last):
            member_copy(p).wait_recv()

    take(0, 1)
    lax.fori_loop(1, 4, take_next, 0)
    take_labels(0)
    score_own(q_own, ql_own, r_own, low)
    take(4, 0)
    member_label_copy().wait_recv()
    widen(ml_par, mlb_par)
    forward_labels(0).wait_recv()
    take(5, 0)
    lax.fori_loop(0, 4, take_forward, 0)
    score_own(q_par, ql_par, r_par, low)
    take(6, 0)
    members_in(0, 2)
    score_pieces(q_own, ql_own, r_own, low, 0, 2)
    score_pieces(q_par, ql_par, r_par, low, 0, 2)
    take(7, 0)
    take_labels(1)
    score_own(q_own, ql_own, r_own, high)
    forward(6).wait_send()
    member_copy(5).start()
    score_pieces(q_own, ql_own, r_own, high, 0, 2)
    members_in(2, 4)
    score_pieces(q_own, ql_own, r_own, whole, 2, 4)
    score_pieces(q_par, ql_par, r_par, low, 2, 4)
    forward_labels(1).wait_recv()
    lax.fori_loop(4, 8, take_forward, 0)
    score_own(q_par, ql_par, r_par, high)
    score_pieces(q_par, ql_par, r_par, high, 0, 4)
    def answer_z(i):
        return pltpu.make_async_remote_copy(
            r_own.at[i], mid_own.at[i], tz_s.at[i], tz_r, device_id=place_at(0, 8 - shift(8 * i)[1], 0), device_id_type=MESH
        )

    def answer_x(i):
        there = place_at(0, 8 - shift(8 * i)[1], 0)[0] if i else ex
        return pltpu.make_async_remote_copy(
            r_par.at[i], mid_par.at[i], b_s.at[i], b_r, device_id=(there, q_mate), device_id_type=MESH
        )

    def answer_y(k):
        return pltpu.make_async_remote_copy(
            ret_mid, ret_in.at[k], t_s.at[k], t_r, device_id=place_at(4 - k // 2, 0, 2 - k % 2), device_id_type=MESH
        )

    for p in range(4, PIECES):
        members_in(p, p + 1)
        score_pieces(q_par, ql_par, r_par, whole, p, p + 1)
        if p == PIECES - 1:
            for i in range(8):
                answer_x(i).start()
        score_pieces(q_own, ql_own, r_own, whole, p, p + 1)

    def columns_of(col_ref, b):
        return jnp.max(col_ref[b * 128 : (b + 1) * 128, :].T, axis=0, keepdims=True)

    for i in range(1, 8):
        answer_z(i).start()
    mid_own[0] = r_own[0]
    blocks = members // 128
    for b in range(blocks):
        c_send[:, b * 128 : (b + 1) * 128] = columns_of(c_par, b)
    columns = pltpu.make_async_remote_copy(c_send, c_got, c_s, c_r, device_id=(ex, m_mate), device_id_type=MESH)
    columns.start()
    far = mid_own.at[pl.ds(1, 7)]
    pltpu.make_async_copy(far, far, tz_r).wait()
    pltpu.make_async_copy(mid_par, mid_par, b_r).wait()
    ret_mid[...] = jnp.maximum(mid_own[...], mid_par[...])
    for k in range(1, 8):
        answer_y(k).start()
    ret_in[0] = ret_mid[...]
    for b in range(blocks):
        rmax_ref[:, b * 128 : (b + 1) * 128] = columns_of(c_own, b)

    by_row = one_hot(iota((64, count), 0) == (dest & 7) * 8 + (dest >> 3))
    answers = ret_in.at[pl.ds(1, 7)]
    pltpu.make_async_copy(answers, answers, t_r).wait()
    by_lane = dot(ret_in[...].reshape(64, 128), by_row, (0, 0), EXACT)
    qmax_ref[...] = jnp.sum(by_lane * is_lane, axis=0, keepdims=True)
    for i in range(8):
        first = 1 if i == 0 else 0
        settle(out, s_sem, i, first)
        settle(lab_out, ls_sem, i, first)
        if i != 6:
            forward(i).wait_send()
    for h in range(2):
        forward_labels(h).wait_send()
    member_label_copy().wait_send()
    for p in range(PIECES):
        member_copy(p).wait_send()
    for i in range(8):
        answer_x(i).wait_send()

    for k in range(1, 8):
        answer_z(k).wait_send()
        answer_y(k).wait_send()
    columns.wait()
    rmax_ref[...] = jnp.maximum(rmax_ref[...], c_got[...])


def shards(embeddings, block_rows, owners, query_cluster, member_cluster):
    members, width = embeddings.shape
    count = block_rows.shape[0]
    vmem = pl.BlockSpec(memory_space=pltpu.VMEM)
    dma = pltpu.SemaphoreType.DMA
    v = pltpu.VMEM
    query_max, resident_max = pl.pallas_call(
        kernel,
        out_shape=(pltpu.VMEM((1, count), F32), pltpu.VMEM((1, members), F32)),
        in_specs=[pl.BlockSpec(memory_space=pl.ANY)] * 5,
        out_specs=(vmem, vmem),
        scratch_shapes=[
            v((count, width), BF16), v((1, count), jnp.int32), v((count // 128, 128), jnp.int32), v((1, members), jnp.int32),
            v((192, 192), BF16), v((192, 192), BF16),
            v((64, 48, 256), BF16), v((64, 48, 256), BF16), v((64, 1, 128), F32), v((64, 1, 128), F32),
            v((768, width), BF16), v((768, width), BF16), v((2, 1, 384), F32), v((2, 1, 384), F32),
            v((members, width), BF16), v((members, width), BF16), v((1, members), F32), v((1, members), F32),
            v((members, 128), F32), v((members, 128), F32),
            v((8, 1, 128), F32), v((8, 1, 128), F32), v((8, 1, 128), F32), v((8, 1, 128), F32),
            v((members, 128), F32), v((members, 128), F32), v((1, members), F32), v((1, members), F32),
            v((8, 1, 128), F32), v((8, 8, 1, 128), F32),
            dma((4 + PIECES,)),
            dma((8,)), dma((8,)), dma((8,)), dma((8,)),
            dma((8,)), dma((8,)), dma((2,)), dma((2,)),
            dma((PIECES,)), dma((PIECES,)), dma, dma,
            dma((8,)), dma, dma, dma, dma((8,)), dma, dma((8,)), dma,
        ],
        compiler_params=pltpu.CompilerParams(collective_id=0, has_side_effects=True, vmem_limit_bytes=56 << 20),
    )(
        embeddings,
        block_rows,
        owners.reshape(1, count),
        query_cluster.reshape(count // 128, 128),
        member_cluster,
    )
    return query_max.reshape(count), resident_max.reshape(members)


def solution(mesh):
    placed = (
        P(("ex", "rep"), None),
        P(("ex", "rep"), None),
        P(("ex", "rep"), None),
        P(("ex", "rep")),
        P("ex", "rep"),
    )
    return jax.shard_map(
        shards,
        mesh=mesh,
        in_specs=placed,
        out_specs=(P(("ex", "rep")), P(("ex", "rep"))),
        check_vma=False,
    )
```
